32 devices in a mesh: polar: 4 (over y, x), azimuth: 8 (over z, core).
Axes of the slice: x: 2, y: 2, z: 4, core: 2. Of those that a mesh axis runs over, the one named last changes fastest.
Arguments:
- state: float32 [2, 32, 72, 1440], P(None, 'polar', None, 'azimuth'), may hold values from -6 to 6
- kernels: float32 [9, 3, 9, 72], replicated, may hold values from -1.25 to 1.25
- kernel_index: int32 [16], replicated, may hold values from 0 to 8
- w_mix: float32 [72, 641], replicated, may hold values from -0.75 to 0.75
- w_in: float32 [641, 1282], replicated, may hold values from -0.25 to 0.25
- b_in: float32 [1282], replicated, may hold values from -4 to 4
- w_out: float32 [1282, 641], replicated, may hold values from -0.15625 to 0.15625
Outputs:
- encoded: float32 [2, 16, 1440, 641], P(None, 'polar', 'azimuth')
The draws below stay inside these ranges and needn't reach their ends.
All inputs are finite; a program needn't handle non-finite values.
Results may differ from the reference program's by a relative error of at most 0.000065.
Values sent between devices are 32-bit elements; how exact they have to be, the bound alone decides.
A program may use at most 64 MiB of HBM per device.

```python
import jax
import jax.numpy as jnp
from jax import lax

FIELDS = 72
LON = 1440
EMBED = 641
FFN = 1282
KERNELS = 9
TAPS = 9
MEMBERS = 2
SPACING = 90
LAT = 32
LAT_OUT = 16


def touch_ends(drawn, rng, smallest, top_value):
    dims = drawn.shape
    index_at = [jax.random.randint(jax.random.fold_in(rng, axis), (), 0, dims[axis]) for axis in range(len(dims))]
    drawn = drawn.at[tuple(index_at)].set(smallest)
    longest = dims.index(max(dims))
    index_at[longest] = (index_at[longest] + 1) % dims[longest]
    return drawn.at[tuple(index_at)].set(top_value)


def block_scale(stream_key, shape, cuts, least, high):
    gain = 1.0
    for axis_at, shards_of in cuts:
        draws = jax.random.uniform(jax.random.fold_in(jax.random.fold_in(stream_key, 6), axis_at), (shards_of,), jnp.float32, least / len(cuts), high / len(cuts))
        gain = gain * jnp.repeat(jnp.exp(draws), shape[axis_at] // shards_of).reshape((-1,) + (1,) * (len(shape) - 1 - axis_at))
    return gain


def noise(stream_key, dims, width, reach, split=(), dtype=jnp.bfloat16):
    loudness = block_scale(stream_key, dims, split, -0.22, 0.18) if split else 1.0
    values = jax.random.normal(stream_key, dims, jnp.float32) * width * loudness
    return jnp.minimum(jnp.maximum(values, -reach), reach).astype(dtype)


def setup_inputs(seed: int = 0) -> dict:
    key_of = jax.random.split(jax.random.key(seed), 8)
    state = noise(key_of[0], (MEMBERS, LAT, FIELDS, LON), 1.0, 6.0, ((1, 4), (3, 8)), jnp.float32)
    kernels = noise(key_of[1], (KERNELS, 3, TAPS, FIELDS), (3 * TAPS) ** -0.5, 1.25, (), jnp.float32)
    kernel_index = touch_ends(jax.random.randint(key_of[2], (LAT_OUT,), 0, KERNELS), jax.random.fold_in(key_of[2], 1), 0, KERNELS - 1).astype(jnp.int32)
    w_mix = noise(key_of[3], (FIELDS, EMBED), FIELDS ** -0.5, 0.75, (), jnp.float32)
    w_in = noise(key_of[4], (EMBED, FFN), EMBED ** -0.5, 0.25, (), jnp.float32)
    b_in = noise(key_of[5], (FFN,), 0.7, 4.0, (), jnp.float32)
    w_out = noise(key_of[6], (FFN, EMBED), FFN ** -0.5, 0.15625, (), jnp.float32)
    return {"state": state, "kernels": kernels, "kernel_index": kernel_index, "w_mix": w_mix, "w_in": w_in, "b_in": b_in, "w_out": w_out}


def reference(state, kernels, kernel_index, w_mix, w_in, b_in, w_out):
    half = TAPS // 2
    taps = kernels[kernel_index]

    def one_member(member):
        padded = jnp.concatenate([jnp.zeros((1, FIELDS, LON), jnp.float32), member], axis=0)
        corr = jnp.zeros((LAT // 2, FIELDS, LON), jnp.float32)
        for tap_lat in range(3):
            rows = padded[tap_lat:tap_lat + LAT:2]
            for tap in range(TAPS):
                shifted = jnp.roll(rows, -(tap - half) * SPACING, axis=2)
                corr = corr + taps[:, tap_lat, tap, :, None] * shifted
        flat = jnp.transpose(corr, (0, 2, 1)).reshape(-1, FIELDS)
        mixed = jnp.dot(flat, w_mix, precision=lax.Precision.HIGHEST, preferred_element_type=jnp.float32)
        pre = jnp.dot(mixed, w_in, precision=lax.Precision.HIGHEST, preferred_element_type=jnp.float32) + b_in
        hidden = jax.nn.gelu(pre, approximate=False)
        out = mixed + jnp.dot(hidden, w_out, precision=lax.Precision.HIGHEST, preferred_element_type=jnp.float32)
        return out.reshape(LAT // 2, LON, EMBED)

    return lax.map(one_member, state)
```

```python
import functools

import jax
import jax.numpy as jnp
from jax import lax
from jax.experimental import pallas as pl
from jax.experimental.pallas import tpu as pltpu
from jax.sharding import PartitionSpec as P

TAPS = 9
SPACING = 90


def shifted(array, axis, by):
    peers = lax.axis_size(axis)
    pairs = [(i, i + by) for i in range(peers) if 0 <= i + by < peers]
    return lax.ppermute(array, axis, pairs)


def row_taps(kernels, kernel_index, out_lat, tap_pos, channel, valid):
    fields = kernels.shape[3]
    total_out = kernel_index.shape[0]
    pick = (out_lat[:, None] == jnp.arange(total_out, dtype=jnp.int32)[None, :]).astype(jnp.int32)
    kernel_of = jnp.sum(pick * kernel_index[None, :], axis=1)
    one_kernel = (
        kernel_of[:, None] == jnp.arange(kernels.shape[0], dtype=jnp.int32)[None, :]
    ).astype(jnp.float32)
    one_tap = (tap_pos[:, None] == jnp.arange(3, dtype=jnp.int32)[None, :]).astype(jnp.float32)
    one_field = (channel[:, None] == jnp.arange(fields, dtype=jnp.int32)[None, :]).astype(
        jnp.float32
    )
    chosen = jnp.einsum(
        "rk,ra,rc,katc->rt",
        one_kernel,
        one_tap,
        one_field,
        kernels,
        precision=lax.Precision.HIGHEST,
        preferred_element_type=jnp.float32,
    )
    return chosen * valid[:, None]


def correlate(cycle, weights):
    half = TAPS // 2
    total = jnp.zeros(cycle.shape, jnp.float32)
    for tap in range(TAPS):
        total = total + weights[:, tap : tap + 1] * jnp.roll(cycle, -(tap - half) * SPACING, axis=1)
    return total


def finish(summed, w_mix, w_in, b_in, w_out):
    lat_half, fields, lon_dev = summed.shape
    mixed = jnp.einsum(
        "ocl,ce->ole",
        summed,
        w_mix,
        precision=lax.Precision.HIGHEST,
        preferred_element_type=jnp.float32,
    ).reshape(lat_half * lon_dev, -1)
    pre = (
        jnp.dot(mixed, w_in, precision=lax.Precision.HIGHEST, preferred_element_type=jnp.float32)
        + b_in
    )
    hidden = jax.nn.gelu(pre, approximate=False)
    out = mixed + jnp.dot(
        hidden, w_out, precision=lax.Precision.HIGHEST, preferred_element_type=jnp.float32
    )
    return out.reshape(lat_half, lon_dev, -1)


def per_device(state, kernels, kernel_index, w_mix, w_in, b_in, w_out):
    members, lat_dev, fields, lon_dev = state.shape
    lat_half = lat_dev // 2
    azim = lax.axis_index("azimuth")
    band = lax.axis_index("polar")
    total_out = kernel_index.shape[0]
    results = []
    for member in range(members):
        block = state[member]
        flat = block.reshape(lat_dev * fields, lon_dev)
        cycle = lax.all_to_all(flat, "azimuth", split_axis=0, concat_axis=1, tiled=True)
        rows_here = cycle.shape[0]
        index = azim * rows_here + jnp.arange(rows_here, dtype=jnp.int32)
        glob = band * lat_dev + index // fields
        channel = index % fields
        parity = glob % 2
        first_w = row_taps(
            kernels,
            kernel_index,
            glob // 2,
            1 + parity,
            channel,
            jnp.ones((rows_here,), jnp.float32),
        )
        second_out = (glob + 1) // 2
        second_ok = ((parity == 1) & (second_out < total_out)).astype(jnp.float32)
        second_w = row_taps(
            kernels, kernel_index, second_out, jnp.zeros_like(glob), channel, second_ok
        )
        planes = jnp.stack([correlate(cycle, first_w), correlate(cycle, second_w)])
        back = lax.all_to_all(planes, "azimuth", split_axis=2, concat_axis=1, tiled=True)
        back = back.reshape(2, lat_half, 2, fields, lon_dev)
        near = back[0, :, 0] + back[0, :, 1]
        upper = back[1, :, 1]
        edge = shifted(upper[-1], "polar", 1)
        summed = near + jnp.concatenate([edge[None], upper[:-1]], axis=0)
        results.append(finish(summed, w_mix, w_in, b_in, w_out))
    return jnp.stack(results)


LANES = 128
SUB = 8
MESH = pl.DeviceIdType.MESH


def halves(x):
    top = x.astype(jnp.bfloat16).astype(jnp.float32)
    return top, x - top


def exchange(
    bands,
    columns,
    idx_ref,
    st,
    kern,
    w_mix,
    w_in,
    b_in,
    w_out,
    corr,
    first,
    rest,
    second,
    peer,
    edge,
    blocks,
    taps,
    own,
    outgoing,
    incoming,
    peer_send,
    peer_recv,
    edge_send,
    edge_recv,
    part_send,
    part_recv,
):
    members, lat_dev, fields, lon_dev = st.shape
    lat_half = lat_dev // 2
    pairs = lat_half // 2
    tiles = fields // SUB
    embed, ffn = w_in.shape
    az = lax.axis_index("azimuth")
    band = lax.axis_index("polar")
    core = lax.rem(az, 2)
    chip = az // 2
    chips = columns // 2
    mate = chip * 2 + 1 - core
    up = lax.rem(chip + 1, chips) * 2 + core
    down = lax.rem(chip + chips - 1, chips) * 2 + core
    next_band = lax.rem(band + 1, bands)
    last_band = lax.rem(band + bands - 1, bands)

    barrier = pltpu.get_barrier_semaphore()
    for who in ((band, mate), (band, up), (band, down), (last_band, az), (last_band, mate)):
        pl.semaphore_signal(barrier, inc=1, device_id=who, device_id_type=MESH)
    pl.semaphore_wait(barrier, 5)

    def remote(src, dst, send, recv, who):
        return pltpu.make_async_remote_copy(
            src_ref=src, dst_ref=dst, send_sem=send, recv_sem=recv, device_id=who, device_id_type=MESH
        )

    peers = [
        remote(st.at[m], peer.at[m], peer_send.at[m], peer_recv.at[m], (band, mate))
        for m in range(members)
    ]
    edges = [
        remote(st.at[:, lat_dev - 1], edge.at[s], edge_send.at[s], edge_recv.at[s], (next_band, who))
        for s, who in enumerate((az, mate))
    ]
    peers[0].start()
    for copy in edges:
        copy.start()
    for copy in peers[1:]:
        copy.start()

    half = TAPS // 2
    pad = half - 1
    for o in range(lat_half):
        k = idx_ref[band * lat_half + o]
        for a in range(3):
            columns_of = kern[k, a].T
            if o == 0 and a == 0:
                columns_of = columns_of * jnp.where(band > 0, 1.0, 0.0)
            for t in range(TAPS):
                taps[o * 3 + a, t + pad] = jnp.broadcast_to(columns_of[:, t : t + 1], (fields, LANES))
            for t in range(pad):
                taps[o * 3 + a, t] = jnp.zeros((fields, LANES), jnp.float32)
                taps[o * 3 + a, t + pad + TAPS] = jnp.zeros((fields, LANES), jnp.float32)

    spare = lon_dev - LANES

    def unpack(src, m, lat, to):
        x = src[:, :LANES]
        y = src[:, LANES:]
        y = jnp.concatenate([y, jnp.zeros((fields, LANES - spare), jnp.float32)], axis=1)
        lane = lax.broadcasted_iota(jnp.int32, x.shape, 1)
        blocks[m, lat, to] = x
        blocks[m, lat, to + 1] = pltpu.roll(jnp.where(lane < SPACING, y, x), LANES - SPACING, 1)

    def pack(value, a_ref, at, pair_of):
        lane = lax.broadcasted_iota(jnp.int32, (SUB, LANES), 1)
        tails = []
        for q in range(2):
            turned = pltpu.roll(value[q][1], SPACING, 1)
            a_ref[at + (q,) + pair_of] = jnp.where(lane < SPACING, value[q][0], turned)
            tails.append(turned)
        a_ref[at + (2,) + pair_of] = jnp.where(
            lane < LANES // 2, tails[0], pltpu.roll(tails[1], LANES // 2, 1)
        )

    def correlate_pair(m, p):
        def body(r, carry):
            rows = pl.ds(pl.multiple_of(r * SUB, SUB), SUB)
            total = [[[None, None] for _ in range(2)] for _ in range(3)]
            for q in range(2):
                o = 2 * p + q
                for a in range(3):
                    x = [blocks[m, 2 * o + a, b, rows, :] for b in range(2 * 2)]
                    for target in range(3):
                        base = pad + half * target - 2 * core
                        w = {d: taps[o * 3 + a, base + d, rows, :] for d in range(-1, 4)}
                        for j in range(2):
                            term = w[-j] * x[0]
                            for b in range(1, 4):
                                term = term + w[b - j] * x[b]
                            old = total[target][q][j]
                            total[target][q][j] = term if old is None else old + term
            pack(total[0], outgoing, (0, m, p), (rows, slice(None)))
            pack(total[1], own, (m, p), (rows, slice(None)))
            pack(total[2], outgoing, (1, m, p), (rows, slice(None)))
            return carry

        lax.fori_loop(0, tiles, body, 0)

    mine = 2 * core
    theirs = 2 - 2 * core
    sends = {}
    for m in range(members):
        for lat in range(lat_dev):
            unpack(st.at[m, lat], m, lat + 1, mine)
        peers[m].wait()
        for lat in range(lat_dev):
            unpack(peer.at[m, lat], m, lat + 1, theirs)
        for p in reversed(range(pairs)):
            if p == 0:
                if m == 0:
                    for copy in edges:
                        copy.wait()
                unpack(edge.at[0, m], m, 0, mine)
                unpack(edge.at[1, m], m, 0, theirs)
            correlate_pair(m, p)
            for way, who in enumerate((up, down)):
                copy = remote(
                    outgoing.at[way, m, p],
                    incoming.at[way, m, p],
                    part_send.at[way, m, p],
                    part_recv.at[way, m, p],
                    (band, who),
                )
                copy.start()
                sends[way, m, p] = copy

    main = ffn // 256 * 256
    extra = ffn - main
    mix_top, mix_low = halves(w_mix[...])
    stacked = jnp.concatenate([mix_top, mix_low], axis=0).astype(jnp.bfloat16)

    def product(cols):
        in_top, in_low = halves(w_in[:, cols])
        big = jnp.dot(stacked, in_top.astype(jnp.bfloat16), preferred_element_type=jnp.float32)
        small = jnp.dot(
            mix_top.astype(jnp.bfloat16), in_low.astype(jnp.bfloat16), preferred_element_type=jnp.float32
        )
        whole = big[:fields] + (big[fields:] + small)
        top, low = halves(whole)
        bias, left = halves(b_in[:, cols])
        bias_low, left = halves(left)
        width = whole.shape[1]
        return jnp.concatenate(
            [top, low, top, bias, bias_low, left, jnp.zeros((256 - 3 * fields - 3, width), jnp.float32)],
            axis=0,
        )

    def fill_first(c, carry):
        cols = pl.ds(pl.multiple_of(c * 256, 256), 256)
        first[:, cols] = product(cols).astype(jnp.bfloat16)
        return carry

    lax.fori_loop(0, main // 256, fill_first, 0)
    tail = product(slice(main, ffn))
    at = 3 * fields + 3
    rest[...] = jnp.concatenate(
        [jnp.zeros((256, at), jnp.float32)]
        + [tail] * 3
        + [jnp.zeros((256, 256 - at - 3 * extra), jnp.float32)],
        axis=1,
    ).astype(jnp.bfloat16)

    def fill_second(c, carry):
        base = pl.multiple_of(c * 256, 256)
        top, low = halves(w_out[pl.ds(base, 256), :])
        second[pl.ds(base, 256), :] = top.astype(jnp.bfloat16)
        second[pl.ds(pl.multiple_of(base + main, 256), 256), :] = low.astype(jnp.bfloat16)
        second[pl.ds(pl.multiple_of(base + 2 * main, 256), 256), :] = top.astype(jnp.bfloat16)
        return carry

    lax.fori_loop(0, main // 256, fill_second, 0)
    top, low = halves(w_out[main:, :])
    second[3 * main :, :] = jnp.concatenate(
        [mix_top, mix_low, mix_top, jnp.zeros((3, embed), jnp.float32), top, low, top]
        + [jnp.zeros((256 - at - 3 * extra, embed), jnp.float32)],
        axis=0,
    ).astype(jnp.bfloat16)

    for m in range(members):
        for p in reversed(range(pairs)):
            for way in range(2):
                sends[way, m, p].wait()
            for q in range(2):
                corr[m, 2 * p + q, :, :LANES] = (
                    own[m, p, q] + incoming[0, m, p, q] + incoming[1, m, p, q]
                )
            tails = own[m, p, 2] + incoming[0, m, p, 2] + incoming[1, m, p, 2]
            corr[m, 2 * p, :, LANES:] = tails[:, :spare]
            corr[m, 2 * p + 1, :, LANES:] = pltpu.roll(tails, LANES // 2, 1)[:, :spare]


def mlp(extra, corr, first, rest, second, out, *scratch):
    group, fields, lon_dev = corr.shape[1:]
    main = first.shape[1]
    room = -(-lon_dev // SUB) * SUB
    low_at = 3 * fields + 3 + 2 * extra
    held = scratch[0]
    lanes = []
    for g in range(group):
        top, low = halves(corr[0, g])
        flat = jnp.concatenate(
            [top, top, low, jnp.ones((3, lon_dev), jnp.float32), jnp.zeros((256 - 3 * fields - 3, lon_dev), jnp.float32)],
            axis=0,
        )
        flat = jnp.concatenate([flat, jnp.zeros((256, 256 - lon_dev), jnp.float32)], axis=1)
        lanes.append(flat.T[:room])
    left = jnp.concatenate(lanes, axis=0)
    left16 = left.astype(jnp.bfloat16)

    def act(weights):
        pre = jnp.dot(left16, weights, preferred_element_type=jnp.float32)
        return pre * 0.5 * (1.0 + lax.erf(pre * (0.5**0.5)))

    for c in range(main // 256):
        hidden = act(first[:, c * 256 : (c + 1) * 256])
        top = hidden.astype(jnp.bfloat16)
        low = (hidden - top.astype(jnp.float32)).astype(jnp.bfloat16)
        held[:, c * 256 : (c + 1) * 256] = top
        held[:, main + c * 256 : main + (c + 1) * 256] = top
        held[:, 2 * main + c * 256 : 2 * main + (c + 1) * 256] = low
    hidden = act(rest[...])
    top, low = halves(hidden)
    lane = lax.broadcasted_iota(jnp.int32, left.shape, 1)
    mixed = jnp.where(
        lane < low_at - 2 * extra, left, jnp.where(lane < low_at, top, jnp.where(lane < low_at + extra, low, 0.0))
    )
    held[:, 3 * main :] = mixed.astype(jnp.bfloat16)
    total = jnp.dot(held[...], second[...], preferred_element_type=jnp.float32)
    for g in range(group):
        out[0, g] = total[g * room : g * room + lon_dev]


def per_device_fast(bands, columns, state, kernels, kernel_index, w_mix, w_in, b_in, w_out):
    members, lat_dev, fields, lon_dev = state.shape
    lat_half = lat_dev // 2
    pairs = lat_half // 2
    embed, ffn = w_in.shape
    main = ffn // 256 * 256
    depth = 3 * main + 256
    vmem = pl.BlockSpec(memory_space=pltpu.VMEM)
    f32 = jnp.float32
    dma = pltpu.SemaphoreType.DMA
    corr, first, rest, second = pl.pallas_call(
        functools.partial(exchange, bands, columns),
        out_shape=(
            jax.ShapeDtypeStruct((members, lat_half, fields, lon_dev), f32),
            jax.ShapeDtypeStruct((256, main), jnp.bfloat16),
            jax.ShapeDtypeStruct((256, 256), jnp.bfloat16),
            jax.ShapeDtypeStruct((depth, embed), jnp.bfloat16),
        ),
        in_specs=[pl.BlockSpec(memory_space=pltpu.SMEM)] + [vmem] * 6,
        out_specs=(vmem,) * 4,
        scratch_shapes=[
            pltpu.VMEM(state.shape, f32),
            pltpu.VMEM((2, members, fields, lon_dev), f32),
            pltpu.VMEM((members, lat_dev + 1, 4, fields, LANES), f32),
            pltpu.VMEM((lat_half * 3, 3 * TAPS // 2 + 2, fields, LANES), f32),
            pltpu.VMEM((members, pairs, 3, fields, LANES), f32),
            pltpu.VMEM((2, members, pairs, 3, fields, LANES), f32),
            pltpu.VMEM((2, members, pairs, 3, fields, LANES), f32),
            dma((members,)),
            dma((members,)),
            dma((2,)),
            dma((2,)),
            dma((2, members, pairs)),
            dma((2, members, pairs)),
        ],
        compiler_params=pltpu.CompilerParams(
            collective_id=0, has_side_effects=True, vmem_limit_bytes=56 * 2**20
        ),
        name="exchange",
    )(kernel_index, state, kernels, w_mix, w_in, b_in[None], w_out)
    group = 2
    room = -(-lon_dev // SUB) * SUB
    whole = lambda x: pl.BlockSpec(x.shape, lambda m, p: (0, 0))
    return pl.pallas_call(
        functools.partial(mlp, ffn - main),
        grid=(members, lat_half // group),
        out_shape=jax.ShapeDtypeStruct((members, lat_half, lon_dev, embed), f32),
        in_specs=[
            pl.BlockSpec((1, group, fields, lon_dev), lambda m, p: (m, p, 0, 0)),
            whole(first),
            whole(rest),
            whole(second),
        ],
        out_specs=pl.BlockSpec((1, group, lon_dev, embed), lambda m, p: (m, p, 0, 0)),
        scratch_shapes=[pltpu.VMEM((group * room, depth), jnp.bfloat16)],
        compiler_params=pltpu.CompilerParams(vmem_limit_bytes=56 * 2**20),
        name="mlp",
    )(corr, first, rest, second)


def fits(mesh, state, w_in):
    bands, columns = mesh.shape["polar"], mesh.shape["azimuth"]
    members, lat, fields, lon = state.shape
    main = w_in.shape[1] // 256 * 256
    return (
        bands >= 2
        and columns % 2 == 0
        and columns >= 6
        and lon == 2 * SPACING * columns
        and lat % (4 * bands) == 0
        and fields % SUB == 0
        and main > 0
        and 3 * fields + 3 + 3 * (w_in.shape[1] - main) <= 256
    )


def solution(mesh):
    placed = (P(None, "polar", None, "azimuth"), P(), P(), P(), P(), P(), P())

    def run(state, kernels, kernel_index, w_mix, w_in, b_in, w_out):
        body = per_device
        if fits(mesh, state, w_in):
            body = functools.partial(per_device_fast, mesh.shape["polar"], mesh.shape["azimuth"])
        return jax.shard_map(
            body,
            mesh=mesh,
            in_specs=placed,
            out_specs=P(None, "polar", "azimuth", None),
            check_vma=False,
        )(state, kernels, kernel_index, w_mix, w_in, b_in, w_out)

    return run
```

```python
import functools

import jax
import jax.numpy as jnp
from jax import lax
from jax.experimental import pallas as pl
from jax.experimental.pallas import tpu as pltpu
from jax.sharding import PartitionSpec as P

TAPS = 9
SPACING = 90


def shifted(array, axis, by):
    peers = lax.axis_size(axis)
    pairs = [(i, i + by) for i in range(peers) if 0 <= i + by < peers]
    return lax.ppermute(array, axis, pairs)


def row_taps(kernels, kernel_index, out_lat, tap_pos, channel, valid):
    fields = kernels.shape[3]
    total_out = kernel_index.shape[0]
    pick = (out_lat[:, None] == jnp.arange(total_out, dtype=jnp.int32)[None, :]).astype(jnp.int32)
    kernel_of = jnp.sum(pick * kernel_index[None, :], axis=1)
    one_kernel = (
        kernel_of[:, None] == jnp.arange(kernels.shape[0], dtype=jnp.int32)[None, :]
    ).astype(jnp.float32)
    one_tap = (tap_pos[:, None] == jnp.arange(3, dtype=jnp.int32)[None, :]).astype(jnp.float32)
    one_field = (channel[:, None] == jnp.arange(fields, dtype=jnp.int32)[None, :]).astype(
        jnp.float32
    )
    chosen = jnp.einsum(
        "rk,ra,rc,katc->rt",
        one_kernel,
        one_tap,
        one_field,
        kernels,
        precision=lax.Precision.HIGHEST,
        preferred_element_type=jnp.float32,
    )
    return chosen * valid[:, None]


def correlate(cycle, weights):
    half = TAPS // 2
    total = jnp.zeros(cycle.shape, jnp.float32)
    for tap in range(TAPS):
        total = total + weights[:, tap : tap + 1] * jnp.roll(cycle, -(tap - half) * SPACING, axis=1)
    return total


def finish(summed, w_mix, w_in, b_in, w_out):
    lat_half, fields, lon_dev = summed.shape
    mixed = jnp.einsum(
        "ocl,ce->ole",
        summed,
        w_mix,
        precision=lax.Precision.HIGHEST,
        preferred_element_type=jnp.float32,
    ).reshape(lat_half * lon_dev, -1)
    pre = (
        jnp.dot(mixed, w_in, precision=lax.Precision.HIGHEST, preferred_element_type=jnp.float32)
        + b_in
    )
    hidden = jax.nn.gelu(pre, approximate=False)
    out = mixed + jnp.dot(
        hidden, w_out, precision=lax.Precision.HIGHEST, preferred_element_type=jnp.float32
    )
    return out.reshape(lat_half, lon_dev, -1)


def per_device(state, kernels, kernel_index, w_mix, w_in, b_in, w_out):
    members, lat_dev, fields, lon_dev = state.shape
    lat_half = lat_dev // 2
    azim = lax.axis_index("azimuth")
    band = lax.axis_index("polar")
    total_out = kernel_index.shape[0]
    results = []
    for member in range(members):
        block = state[member]
        flat = block.reshape(lat_dev * fields, lon_dev)
        cycle = lax.all_to_all(flat, "azimuth", split_axis=0, concat_axis=1, tiled=True)
        rows_here = cycle.shape[0]
        index = azim * rows_here + jnp.arange(rows_here, dtype=jnp.int32)
        glob = band * lat_dev + index // fields
        channel = index % fields
        parity = glob % 2
        first_w = row_taps(
            kernels,
            kernel_index,
            glob // 2,
            1 + parity,
            channel,
            jnp.ones((rows_here,), jnp.float32),
        )
        second_out = (glob + 1) // 2
        second_ok = ((parity == 1) & (second_out < total_out)).astype(jnp.float32)
        second_w = row_taps(
            kernels, kernel_index, second_out, jnp.zeros_like(glob), channel, second_ok
        )
        planes = jnp.stack([correlate(cycle, first_w), correlate(cycle, second_w)])
        back = lax.all_to_all(planes, "azimuth", split_axis=2, concat_axis=1, tiled=True)
        back = back.reshape(2, lat_half, 2, fields, lon_dev)
        near = back[0, :, 0] + back[0, :, 1]
        upper = back[1, :, 1]
        edge = shifted(upper[-1], "polar", 1)
        summed = near + jnp.concatenate([edge[None], upper[:-1]], axis=0)
        results.append(finish(summed, w_mix, w_in, b_in, w_out))
    return jnp.stack(results)


LANES = 128
SUB = 8
GROUP = 4
WIDE = 256
EARLY = 3
MESH = pl.DeviceIdType.MESH


def halves(x):
    top = x.astype(jnp.bfloat16).astype(jnp.float32)
    return top, x - top


def room_of(lon_dev):
    return -(-(lon_dev // 2 * GROUP) // 16) * 16


def mlp_rows(fields, extra, left16, first, rest, second, held):
    main = first.shape[1]
    at = 3 * fields + 3
    low_at = at + 2 * extra

    def act(weights):
        pre = jnp.dot(left16, weights, preferred_element_type=jnp.float32)
        return pre * 0.5 * (1.0 + lax.erf(pre * (0.5**0.5)))

    for c in range(main // WIDE):
        hidden = act(first[:, c * WIDE : (c + 1) * WIDE])
        top = hidden.astype(jnp.bfloat16)
        low = (hidden - top.astype(jnp.float32)).astype(jnp.bfloat16)
        held[:, c * WIDE : (c + 1) * WIDE] = top
        held[:, main + c * WIDE : main + (c + 1) * WIDE] = top
        held[:, 2 * main + c * WIDE : 2 * main + (c + 1) * WIDE] = low
    top, low = halves(act(rest[...]))
    lane = lax.broadcasted_iota(jnp.int32, top.shape, 1)
    mixed = jnp.where(
        lane < at,
        left16.astype(jnp.float32),
        jnp.where(lane < low_at, top, jnp.where(lane < low_at + extra, low, 0.0)),
    )
    held[:, 3 * main :] = mixed.astype(jnp.bfloat16)
    return lambda: jnp.dot(held[...], second[...], preferred_element_type=jnp.float32)


def exchange(
    bands,
    columns,
    early,
    idx_ref,
    kern,
    w_mix,
    b_in,
    st_hbm,
    w_in_hbm,
    w_out_hbm,
    left_out,
    first_out,
    rest_out,
    second_out,
    early_out,
    st,
    w_in,
    w_out,
    first,
    rest,
    second,
    left,
    rows_f32,
    held,
    result,
    peer,
    edge,
    blocks,
    taps,
    own,
    outgoing,
    incoming,
    load_sem,
    store_sem,
    result_sem,
    peer_send,
    peer_recv,
    edge_send,
    edge_recv,
    part_send,
    part_recv,
):
    members, lat_dev, fields, lon_dev = st.shape
    lat_half = lat_dev // 2
    tiles = fields // SUB
    embed, ffn = w_in.shape
    pieces = 2 * members
    az = lax.axis_index("azimuth")
    band = lax.axis_index("polar")
    core = lax.rem(az, 2)
    chip = az // 2
    chips = columns // 2
    mate = chip * 2 + 1 - core
    up = lax.rem(chip + 1, chips) * 2 + core
    down = lax.rem(chip + chips - 1, chips) * 2 + core
    next_band = lax.rem(band + 1, bands)
    last_band = lax.rem(band + bands - 1, bands)

    loads = [pltpu.make_async_copy(st_hbm.at[m], st.at[m], load_sem.at[m]) for m in range(members)]
    load_in = pltpu.make_async_copy(w_in_hbm, w_in, load_sem.at[members])
    load_out = pltpu.make_async_copy(w_out_hbm, w_out, load_sem.at[members + 1])
    for copy in loads:
        copy.start()

    barrier = pltpu.get_barrier_semaphore()
    for who in ((band, mate), (band, up), (band, down), (last_band, az), (last_band, mate)):
        pl.semaphore_signal(barrier, inc=1, device_id=who, device_id_type=MESH)
    pl.semaphore_wait(barrier, 5)

    def remote(src, dst, send, recv, who):
        return pltpu.make_async_remote_copy(
            src_ref=src, dst_ref=dst, send_sem=send, recv_sem=recv, device_id=who, device_id_type=MESH
        )

    peers = []
    edges = []
    for m in range(members):
        peers.append(remote(st_hbm.at[m], peer.at[m], peer_send.at[m], peer_recv.at[m], (band, mate)))
        edges.append(
            [
                remote(
                    st_hbm.at[m, lat_dev - 1],
                    edge.at[s, m],
                    edge_send.at[s, m],
                    edge_recv.at[s, m],
                    (next_band, who),
                )
                for s, who in enumerate((az, mate))
            ]
        )
    for m in range(members):
        for copy in edges[m]:
            copy.start()
        peers[m].start()
    load_in.start()
    load_out.start()

    half = TAPS // 2
    pad = half - 1
    for o in range(lat_half):
        k = idx_ref[band * lat_half + o]
        for a in range(3):
            columns_of = kern[k, :, a, :].T
            if o == 0 and a == 0:
                columns_of = columns_of * jnp.where(band > 0, 1.0, 0.0)
            for t in range(TAPS):
                taps[o * 3 + a, t + pad] = jnp.broadcast_to(columns_of[:, t : t + 1], (fields, LANES))
            for t in range(pad):
                taps[o * 3 + a, t] = jnp.zeros((fields, LANES), jnp.float32)
                taps[o * 3 + a, t + pad + TAPS] = jnp.zeros((fields, LANES), jnp.float32)

    spare = lon_dev - LANES

    def unpack(src, m, lat, to):
        x = src[:, :LANES]
        y = src[:, LANES:]
        y = jnp.concatenate([y, jnp.zeros((fields, LANES - spare), jnp.float32)], axis=1)
        lane = lax.broadcasted_iota(jnp.int32, x.shape, 1)
        blocks[m, lat, to] = x
        blocks[m, lat, to + 1] = pltpu.roll(jnp.where(lane < SPACING, y, x), LANES - SPACING, 1)

    turns = [q * SPACING % LANES for q in range(GROUP)]

    def pack(value, ref, at, rows):
        lane = lax.broadcasted_iota(jnp.int32, (SUB, LANES), 1)
        turned = [value[0]] + [pltpu.roll(value[q], turns[q], 1) for q in range(1, GROUP)]
        ref[at + (0, rows, slice(None))] = jnp.where(lane < turns[1], turned[0], turned[1])
        ref[at + (1, rows, slice(None))] = jnp.where(lane < turns[2], turned[1], turned[2])
        ref[at + (2, rows, slice(None))] = jnp.where(lane < turns[3], turned[2], turned[3])

    def correlate_member(m):
        def body(r, carry):
            rows = pl.ds(pl.multiple_of(r * SUB, SUB), SUB)
            total = [[[None] * lat_half for _ in range(2)] for _ in range(3)]
            for o in range(lat_half):
                for a in range(3):
                    x = [blocks[m, 2 * o + a, b, rows, :] for b in range(4)]
                    for target in range(3):
                        base = pad + half * target - 2 * core
                        w = {d: taps[o * 3 + a, base + d, rows, :] for d in range(-1, 4)}
                        for j in range(2):
                            term = w[-j] * x[0]
                            for b in range(1, 4):
                                term = term + w[b - j] * x[b]
                            old = total[target][j][o]
                            total[target][j][o] = term if old is None else old + term
            for j in range(2):
                pack(total[0][j], outgoing, (0, 2 * m + j), rows)
                pack(total[1][j], own, (2 * m + j,), rows)
                pack(total[2][j], outgoing, (1, 2 * m + j), rows)
            return carry

        lax.fori_loop(0, tiles, body, 0)

    def parts(k):
        return [
            remote(
                outgoing.at[way, k],
                incoming.at[way, k],
                part_send.at[way, k],
                part_recv.at[way, k],
                (band, who),
            )
            for way, who in enumerate((up, down))
        ]

    mine = 2 * core
    theirs = 2 - 2 * core
    for m in range(members):
        loads[m].wait()
        for lat in range(lat_dev):
            unpack(st.at[m, lat], m, lat + 1, mine)
        peers[m].wait()
        for lat in range(lat_dev):
            unpack(peer.at[m, lat], m, lat + 1, theirs)
        for copy in edges[m]:
            copy.wait()
        unpack(edge.at[0, m], m, 0, mine)
        unpack(edge.at[1, m], m, 0, theirs)
        correlate_member(m)
        for j in range(2):
            for copy in parts(2 * m + j):
                copy.start()

    main = ffn // WIDE * WIDE
    extra = ffn - main
    at = 3 * fields + 3
    mix_top, mix_low = halves(w_mix[...])
    stacked = jnp.concatenate([mix_top, mix_low], axis=0).astype(jnp.bfloat16)
    load_in.wait()

    def product(cols):
        in_top, in_low = halves(w_in[:, cols])
        big = jnp.dot(stacked, in_top.astype(jnp.bfloat16), preferred_element_type=jnp.float32)
        small = jnp.dot(
            mix_top.astype(jnp.bfloat16), in_low.astype(jnp.bfloat16), preferred_element_type=jnp.float32
        )
        whole = big[:fields] + (big[fields:] + small)
        top, low = halves(whole)
        bias, leave = halves(b_in[cols][None, :])
        bias_low, leave = halves(leave)
        width = whole.shape[1]
        return jnp.concatenate(
            [top, low, top, bias, bias_low, leave, jnp.zeros((WIDE - at, width), jnp.float32)], axis=0
        )

    for c in range(main // WIDE):
        cols = slice(c * WIDE, (c + 1) * WIDE)
        first[:, cols] = product(cols).astype(jnp.bfloat16)
    tail = product(slice(main, ffn))
    rest[...] = jnp.concatenate(
        [jnp.zeros((WIDE, at), jnp.float32)]
        + [tail] * 3
        + [jnp.zeros((WIDE, WIDE - at - 3 * extra), jnp.float32)],
        axis=1,
    ).astype(jnp.bfloat16)
    load_out.wait()
    for c in range(main // WIDE):
        top, low = halves(w_out[:, c * WIDE : (c + 1) * WIDE].T)
        base = c * WIDE
        second[base : base + WIDE, :] = top.astype(jnp.bfloat16)
        second[base + main : base + main + WIDE, :] = low.astype(jnp.bfloat16)
        second[base + 2 * main : base + 2 * main + WIDE, :] = top.astype(jnp.bfloat16)
    top, low = halves(w_out[:, main:].T)
    second[3 * main :, :] = jnp.concatenate(
        [mix_top, mix_low, mix_top, jnp.zeros((3, embed), jnp.float32), top, low, top]
        + [jnp.zeros((WIDE - at - 3 * extra, embed), jnp.float32)],
        axis=0,
    ).astype(jnp.bfloat16)
    stores = [
        pltpu.make_async_copy(src, dst, store_sem.at[i])
        for i, (src, dst) in enumerate(((first, first_out), (rest, rest_out), (second, second_out)))
    ]
    for copy in stores:
        copy.start()

    count = lon_dev // 2
    room = rows_f32.shape[1]
    for side in range(WIDE // LANES):
        rows_f32[side, count * GROUP :, :] = jnp.zeros((room - count * GROUP, LANES), jnp.float32)

    def finish_part(k):
        for copy in parts(k):
            copy.wait()
        v = [own[k, i] + incoming[0, k, i] + incoming[1, k, i] for i in range(GROUP - 1)]
        lane = lax.broadcasted_iota(jnp.int32, v[0].shape, 1)
        fields_of = [v[0]]
        for q in range(1, GROUP):
            both = v[q - 1] if q == GROUP - 1 else jnp.where(lane >= turns[q], v[q - 1], v[q])
            fields_of.append(pltpu.roll(both, LANES - turns[q], 1))
        for q in range(GROUP):
            top, low = halves(fields_of[q])
            flat = jnp.concatenate(
                [top, top, low, jnp.ones((3, LANES), jnp.float32)]
                + [jnp.zeros((WIDE - at, LANES), jnp.float32)],
                axis=0,
            )
            turned = flat.T[:count]
            for side in range(WIDE // LANES):
                rows_f32[side, pl.ds(q, count, stride=GROUP), :] = turned[
                    :, side * LANES : (side + 1) * LANES
                ]
        return jnp.concatenate([rows_f32[side] for side in range(WIDE // LANES)], axis=1).astype(
            jnp.bfloat16
        )

    def early_piece(k, carry):
        left[...] = finish_part(k)
        total = mlp_rows(fields, extra, left[...], first, rest, second, held)()
        result[...] = total[: count * GROUP].reshape(count, GROUP, embed)
        copy = pltpu.make_async_copy(result, early_out.at[k], result_sem)
        copy.start()
        copy.wait()
        return carry

    if early:
        lax.fori_loop(0, early, early_piece, 0)
    for k in range(early, pieces):
        left_out[k - early] = finish_part(k)
    for copy in stores:
        copy.wait()


def mlp(
    fields, extra, early, left_ref, first, rest, second_hbm, early_in, out, second, held, result, load_sem, move_sem, result_sem
):
    late = left_ref.shape[0]
    count = result.shape[0]
    embed = result.shape[2]
    load = pltpu.make_async_copy(second_hbm, second, load_sem)
    load.start()
    moves = [
        pltpu.make_async_copy(
            early_in.at[k], out.at[k // 2, pl.ds(k % 2 * count, count)], move_sem.at[k]
        )
        for k in range(early)
    ]
    for copy in moves:
        copy.start()
    for i in range(late):
        k = early + i
        finish = mlp_rows(fields, extra, left_ref[i], first, rest, second, held)
        if i == 0:
            load.wait()
        result[...] = finish()[: count * GROUP].reshape(count, GROUP, embed)
        copy = pltpu.make_async_copy(
            result, out.at[k // 2, pl.ds(k % 2 * count, count)], result_sem
        )
        copy.start()
        copy.wait()
    for copy in moves:
        copy.wait()


def per_device_fast(bands, columns, state, kernels, kernel_index, w_mix, w_in, b_in, w_out):
    members, lat_dev, fields, lon_dev = state.shape
    lat_half = lat_dev // 2
    pieces = 2 * members
    early = min(EARLY, pieces - 1)
    late = pieces - early
    count = lon_dev // 2
    embed, ffn = w_in.shape
    main = ffn // WIDE * WIDE
    depth = 3 * main + WIDE
    room = room_of(lon_dev)
    vmem = pl.BlockSpec(memory_space=pltpu.VMEM)
    hbm = pl.BlockSpec(memory_space=pl.ANY)
    f32 = jnp.float32
    half = jnp.bfloat16
    dma = pltpu.SemaphoreType.DMA
    packed = (pieces, GROUP - 1, fields, LANES)
    left, first, rest, second, ready = pl.pallas_call(
        functools.partial(exchange, bands, columns, early),
        out_shape=(
            jax.ShapeDtypeStruct((late, room, WIDE), half),
            jax.ShapeDtypeStruct((WIDE, main), half),
            jax.ShapeDtypeStruct((WIDE, WIDE), half),
            jax.ShapeDtypeStruct((depth, embed), half),
            jax.ShapeDtypeStruct((early, count, GROUP, embed), f32),
        ),
        in_specs=[pl.BlockSpec(memory_space=pltpu.SMEM)] + [vmem] * 3 + [hbm] * 3,
        out_specs=(vmem,) + (hbm,) * 4,
        scratch_shapes=[
            pltpu.VMEM(state.shape, f32),
            pltpu.VMEM(w_in.shape, f32),
            pltpu.VMEM(w_out.shape[::-1], f32),
            pltpu.VMEM((WIDE, main), half),
            pltpu.VMEM((WIDE, WIDE), half),
            pltpu.VMEM((depth, embed), half),
            pltpu.VMEM((room, WIDE), half),
            pltpu.VMEM((WIDE // LANES, room, LANES), f32),
            pltpu.VMEM((room, depth), half),
            pltpu.VMEM((count, GROUP, embed), f32),
            pltpu.VMEM(state.shape, f32),
            pltpu.VMEM((2, members, fields, lon_dev), f32),
            pltpu.VMEM((members, lat_dev + 1, 4, fields, LANES), f32),
            pltpu.VMEM((lat_half * 3, 2 * TAPS - 3, fields, LANES), f32),
            pltpu.VMEM(packed, f32),
            pltpu.VMEM((2,) + packed, f32),
            pltpu.VMEM((2,) + packed, f32),
            dma((members + 2,)),
            dma((3,)),
            dma(()),
            dma((members,)),
            dma((members,)),
            dma((2, members)),
            dma((2, members)),
            dma((2, pieces)),
            dma((2, pieces)),
        ],
        compiler_params=pltpu.CompilerParams(
            collective_id=0, has_side_effects=True, vmem_limit_bytes=60 * 2**20
        ),
        name="exchange",
    )(
        kernel_index,
        jnp.transpose(kernels, (0, 2, 1, 3)),
        w_mix,
        b_in,
        state,
        w_in,
        w_out.T,
    )
    out = pl.pallas_call(
        functools.partial(mlp, fields, ffn - main, early),
        out_shape=jax.ShapeDtypeStruct((members, lon_dev, lat_half, embed), f32),
        in_specs=[vmem] * 3 + [hbm] * 2,
        out_specs=hbm,
        scratch_shapes=[
            pltpu.VMEM((depth, embed), half),
            pltpu.VMEM((room, depth), half),
            pltpu.VMEM((count, GROUP, embed), f32),
            dma(()),
            dma((early,)),
            dma(()),
        ],
        compiler_params=pltpu.CompilerParams(vmem_limit_bytes=56 * 2**20),
        name="mlp",
    )(left, first, rest, second, ready)
    return jnp.transpose(out, (0, 2, 1, 3))


def fits(mesh, state, w_in):
    bands, columns = mesh.shape["polar"], mesh.shape["azimuth"]
    members, lat, fields, lon = state.shape
    main = w_in.shape[1] // WIDE * WIDE
    return (
        bands >= 2
        and columns % 2 == 0
        and columns >= 6
        and lon == 2 * SPACING * columns
        and lat == 2 * GROUP * bands
        and fields % SUB == 0
        and main > 0
        and 3 * fields + 3 + 3 * (w_in.shape[1] - main) <= WIDE
    )


def solution(mesh):
    placed = (P(None, "polar", None, "azimuth"), P(), P(), P(), P(), P(), P())

    def run(state, kernels, kernel_index, w_mix, w_in, b_in, w_out):
        body = per_device
        if fits(mesh, state, w_in):
            body = functools.partial(per_device_fast, mesh.shape["polar"], mesh.shape["azimuth"])
        return jax.shard_map(
            body,
            mesh=mesh,
            in_specs=placed,
            out_specs=P(None, "polar", "azimuth", None),
            check_vma=False,
        )(state, kernels, kernel_index, w_mix, w_in, b_in, w_out)

    return run
```

```python
import functools

import jax
import jax.numpy as jnp
from jax import lax
from jax.experimental import pallas as pl
from jax.experimental.pallas import tpu as pltpu
from jax.sharding import PartitionSpec as P

TAPS = 9
SPACING = 90


def shifted(array, axis, by):
    peers = lax.axis_size(axis)
    pairs = [(i, i + by) for i in range(peers) if 0 <= i + by < peers]
    return lax.ppermute(array, axis, pairs)


def row_taps(kernels, kernel_index, out_lat, tap_pos, channel, valid):
    fields = kernels.shape[3]
    total_out = kernel_index.shape[0]
    pick = (out_lat[:, None] == jnp.arange(total_out, dtype=jnp.int32)[None, :]).astype(jnp.int32)
    kernel_of = jnp.sum(pick * kernel_index[None, :], axis=1)
    one_kernel = (
        kernel_of[:, None] == jnp.arange(kernels.shape[0], dtype=jnp.int32)[None, :]
    ).astype(jnp.float32)
    one_tap = (tap_pos[:, None] == jnp.arange(3, dtype=jnp.int32)[None, :]).astype(jnp.float32)
    one_field = (channel[:, None] == jnp.arange(fields, dtype=jnp.int32)[None, :]).astype(
        jnp.float32
    )
    chosen = jnp.einsum(
        "rk,ra,rc,katc->rt",
        one_kernel,
        one_tap,
        one_field,
        kernels,
        precision=lax.Precision.HIGHEST,
        preferred_element_type=jnp.float32,
    )
    return chosen * valid[:, None]


def correlate(cycle, weights):
    half = TAPS // 2
    total = jnp.zeros(cycle.shape, jnp.float32)
    for tap in range(TAPS):
        total = total + weights[:, tap : tap + 1] * jnp.roll(cycle, -(tap - half) * SPACING, axis=1)
    return total


def finish(summed, w_mix, w_in, b_in, w_out):
    lat_half, fields, lon_dev = summed.shape
    mixed = jnp.einsum(
        "ocl,ce->ole",
        summed,
        w_mix,
        precision=lax.Precision.HIGHEST,
        preferred_element_type=jnp.float32,
    ).reshape(lat_half * lon_dev, -1)
    pre = (
        jnp.dot(mixed, w_in, precision=lax.Precision.HIGHEST, preferred_element_type=jnp.float32)
        + b_in
    )
    hidden = jax.nn.gelu(pre, approximate=False)
    out = mixed + jnp.dot(
        hidden, w_out, precision=lax.Precision.HIGHEST, preferred_element_type=jnp.float32
    )
    return out.reshape(lat_half, lon_dev, -1)


def per_device(state, kernels, kernel_index, w_mix, w_in, b_in, w_out):
    members, lat_dev, fields, lon_dev = state.shape
    lat_half = lat_dev // 2
    azim = lax.axis_index("azimuth")
    band = lax.axis_index("polar")
    total_out = kernel_index.shape[0]
    results = []
    for member in range(members):
        block = state[member]
        flat = block.reshape(lat_dev * fields, lon_dev)
        cycle = lax.all_to_all(flat, "azimuth", split_axis=0, concat_axis=1, tiled=True)
        rows_here = cycle.shape[0]
        index = azim * rows_here + jnp.arange(rows_here, dtype=jnp.int32)
        glob = band * lat_dev + index // fields
        channel = index % fields
        parity = glob % 2
        first_w = row_taps(
            kernels,
            kernel_index,
            glob // 2,
            1 + parity,
            channel,
            jnp.ones((rows_here,), jnp.float32),
        )
        second_out = (glob + 1) // 2
        second_ok = ((parity == 1) & (second_out < total_out)).astype(jnp.float32)
        second_w = row_taps(
            kernels, kernel_index, second_out, jnp.zeros_like(glob), channel, second_ok
        )
        planes = jnp.stack([correlate(cycle, first_w), correlate(cycle, second_w)])
        back = lax.all_to_all(planes, "azimuth", split_axis=2, concat_axis=1, tiled=True)
        back = back.reshape(2, lat_half, 2, fields, lon_dev)
        near = back[0, :, 0] + back[0, :, 1]
        upper = back[1, :, 1]
        edge = shifted(upper[-1], "polar", 1)
        summed = near + jnp.concatenate([edge[None], upper[:-1]], axis=0)
        results.append(finish(summed, w_mix, w_in, b_in, w_out))
    return jnp.stack(results)


LANES = 128
SUB = 8
GROUP = 4
WIDE = 256
EARLY = 3
MESH = pl.DeviceIdType.MESH


def halves(x):
    top = x.astype(jnp.bfloat16).astype(jnp.float32)
    return top, x - top


def room_of(lon_dev):
    return -(-(lon_dev // 2 * GROUP) // 16) * 16


def mlp_rows(fields, extra, left16, first, rest, second, held):
    main = first.shape[1]
    at = 3 * fields + 3
    low_at = at + 2 * extra

    def act(weights):
        pre = jnp.dot(left16, weights, preferred_element_type=jnp.float32)
        return pre * 0.5 * (1.0 + lax.erf(pre * (0.5**0.5)))

    for c in range(main // WIDE):
        hidden = act(first[:, c * WIDE : (c + 1) * WIDE])
        top = hidden.astype(jnp.bfloat16)
        low = (hidden - top.astype(jnp.float32)).astype(jnp.bfloat16)
        held[:, c * WIDE : (c + 1) * WIDE] = top
        held[:, main + c * WIDE : main + (c + 1) * WIDE] = top
        held[:, 2 * main + c * WIDE : 2 * main + (c + 1) * WIDE] = low
    top, low = halves(act(rest[...]))
    lane = lax.broadcasted_iota(jnp.int32, top.shape, 1)
    mixed = jnp.where(
        lane < at,
        left16.astype(jnp.float32),
        jnp.where(lane < low_at, top, jnp.where(lane < low_at + extra, low, 0.0)),
    )
    held[:, 3 * main :] = mixed.astype(jnp.bfloat16)
    return lambda: jnp.dot(held[...], second[...], preferred_element_type=jnp.float32)


def exchange(
    bands,
    columns,
    early,
    idx_ref,
    kern,
    w_mix,
    b_in,
    st_hbm,
    w_in_hbm,
    w_out_hbm,
    left_out,
    first_out,
    rest_out,
    second_out,
    early_out,
    st,
    w_in,
    w_out,
    first,
    rest,
    second,
    left,
    rows_f32,
    held,
    result,
    peer,
    edge,
    blocks,
    taps,
    own,
    outgoing,
    incoming,
    load_sem,
    store_sem,
    result_sem,
    peer_send,
    peer_recv,
    edge_send,
    edge_recv,
    part_send,
    part_recv,
):
    members, lat_dev, fields, lon_dev = st.shape
    lat_half = lat_dev // 2
    tiles = fields // SUB
    embed, ffn = w_in.shape
    pieces = 2 * members
    az = lax.axis_index("azimuth")
    band = lax.axis_index("polar")
    core = lax.rem(az, 2)
    chip = az // 2
    chips = columns // 2
    mate = chip * 2 + 1 - core
    up = lax.rem(chip + 1, chips) * 2 + core
    down = lax.rem(chip + chips - 1, chips) * 2 + core
    next_band = lax.rem(band + 1, bands)
    last_band = lax.rem(band + bands - 1, bands)

    loads = [pltpu.make_async_copy(st_hbm.at[m], st.at[m], load_sem.at[m]) for m in range(members)]
    load_in = pltpu.make_async_copy(w_in_hbm, w_in, load_sem.at[members])
    load_out = pltpu.make_async_copy(w_out_hbm, w_out, load_sem.at[members + 1])
    for copy in loads:
        copy.start()

    barrier = pltpu.get_barrier_semaphore()
    for who in ((band, mate), (band, up), (band, down), (last_band, az), (last_band, mate)):
        pl.semaphore_signal(barrier, inc=1, device_id=who, device_id_type=MESH)
    pl.semaphore_wait(barrier, 5)

    def remote(src, dst, send, recv, who):
        return pltpu.make_async_remote_copy(
            src_ref=src, dst_ref=dst, send_sem=send, recv_sem=recv, device_id=who, device_id_type=MESH
        )

    peers = []
    edges = []
    for m in range(members):
        peers.append(remote(st_hbm.at[m], peer.at[m], peer_send.at[m], peer_recv.at[m], (band, mate)))
        edges.append(
            [
                remote(
                    st_hbm.at[m, lat_dev - 1],
                    edge.at[s, m],
                    edge_send.at[s, m],
                    edge_recv.at[s, m],
                    (next_band, who),
                )
                for s, who in enumerate((az, mate))
            ]
        )
    for m in range(members):
        for copy in edges[m]:
            copy.start()
        peers[m].start()
    load_in.start()
    load_out.start()

    half = TAPS // 2
    pad = half - 1
    for o in range(lat_half):
        k = idx_ref[band * lat_half + o]
        for a in range(3):
            columns_of = kern[k, :, a, :].T
            if o == 0 and a == 0:
                columns_of = columns_of * jnp.where(band > 0, 1.0, 0.0)
            for t in range(TAPS):
                taps[o * 3 + a, t + pad] = jnp.broadcast_to(columns_of[:, t : t + 1], (fields, LANES))
            for t in range(pad):
                taps[o * 3 + a, t] = jnp.zeros((fields, LANES), jnp.float32)
                taps[o * 3 + a, t + pad + TAPS] = jnp.zeros((fields, LANES), jnp.float32)

    spare = lon_dev - LANES

    def unpack(src, m, lat, to):
        x = src[:, :LANES]
        y = src[:, LANES:]
        y = jnp.concatenate([y, jnp.zeros((fields, LANES - spare), jnp.float32)], axis=1)
        lane = lax.broadcasted_iota(jnp.int32, x.shape, 1)
        blocks[m, lat, to] = x
        blocks[m, lat, to + 1] = pltpu.roll(jnp.where(lane < SPACING, y, x), LANES - SPACING, 1)

    turns = [q * SPACING % LANES for q in range(GROUP)]

    def pack(value, ref, at, rows):
        lane = lax.broadcasted_iota(jnp.int32, (SUB, LANES), 1)
        turned = [value[0]] + [pltpu.roll(value[q], turns[q], 1) for q in range(1, GROUP)]
        ref[at + (0, rows, slice(None))] = jnp.where(lane < turns[1], turned[0], turned[1])
        ref[at + (1, rows, slice(None))] = jnp.where(lane < turns[2], turned[1], turned[2])
        ref[at + (2, rows, slice(None))] = jnp.where(lane < turns[3], turned[2], turned[3])

    def correlate_member(m):
        def body(r, carry):
            rows = pl.ds(pl.multiple_of(r * SUB, SUB), SUB)
            total = [[[None] * lat_half for _ in range(2)] for _ in range(3)]
            for o in range(lat_half):
                for a in range(3):
                    x = [blocks[m, 2 * o + a, b, rows, :] for b in range(4)]
                    for target in range(3):
                        base = pad + half * target - 2 * core
                        w = {d: taps[o * 3 + a, base + d, rows, :] for d in range(-1, 4)}
                        for j in range(2):
                            term = w[-j] * x[0]
                            for b in range(1, 4):
                                term = term + w[b - j] * x[b]
                            old = total[target][j][o]
                            total[target][j][o] = term if old is None else old + term
            for j in range(2):
                pack(total[0][j], outgoing, (0, 2 * m + j), rows)
                pack(total[1][j], own, (2 * m + j,), rows)
                pack(total[2][j], outgoing, (1, 2 * m + j), rows)
            return carry

        lax.fori_loop(0, tiles, body, 0)

    def parts(k):
        return [
            remote(
                outgoing.at[way, k],
                incoming.at[way, k],
                part_send.at[way, k],
                part_recv.at[way, k],
                (band, who),
            )
            for way, who in enumerate((up, down))
        ]

    mine = 2 * core
    theirs = 2 - 2 * core
    for m in range(members):
        loads[m].wait()
        for lat in range(lat_dev):
            unpack(st.at[m, lat], m, lat + 1, mine)
        peers[m].wait()
        for lat in range(lat_dev):
            unpack(peer.at[m, lat], m, lat + 1, theirs)
        for copy in edges[m]:
            copy.wait()
        unpack(edge.at[0, m], m, 0, mine)
        unpack(edge.at[1, m], m, 0, theirs)
        correlate_member(m)
        for j in range(2):
            for copy in parts(2 * m + j):
                copy.start()

    main = ffn // WIDE * WIDE
    extra = ffn - main
    at = 3 * fields + 3
    mix_top, mix_low = halves(w_mix[...])
    stacked = jnp.concatenate([mix_top, mix_low], axis=0).astype(jnp.bfloat16)
    load_in.wait()

    def product(cols):
        in_top, in_low = halves(w_in[:, cols])
        big = jnp.dot(stacked, in_top.astype(jnp.bfloat16), preferred_element_type=jnp.float32)
        small = jnp.dot(
            mix_top.astype(jnp.bfloat16), in_low.astype(jnp.bfloat16), preferred_element_type=jnp.float32
        )
        whole = big[:fields] + (big[fields:] + small)
        top, low = halves(whole)
        bias, leave = halves(b_in[cols][None, :])
        bias_low, leave = halves(leave)
        width = whole.shape[1]
        return jnp.concatenate(
            [top, low, top, bias, bias_low, leave, jnp.zeros((WIDE - at, width), jnp.float32)], axis=0
        )

    for c in range(main // WIDE):
        cols = slice(c * WIDE, (c + 1) * WIDE)
        first[:, cols] = product(cols).astype(jnp.bfloat16)
    tail = product(slice(main, ffn))
    rest[...] = jnp.concatenate(
        [jnp.zeros((WIDE, at), jnp.float32)]
        + [tail] * 3
        + [jnp.zeros((WIDE, WIDE - at - 3 * extra), jnp.float32)],
        axis=1,
    ).astype(jnp.bfloat16)
    load_out.wait()
    for c in range(main // WIDE):
        top, low = halves(w_out[:, c * WIDE : (c + 1) * WIDE].T)
        base = c * WIDE
        second[base : base + WIDE, :] = top.astype(jnp.bfloat16)
        second[base + main : base + main + WIDE, :] = low.astype(jnp.bfloat16)
        second[base + 2 * main : base + 2 * main + WIDE, :] = top.astype(jnp.bfloat16)
    top, low = halves(w_out[:, main:].T)
    second[3 * main :, :] = jnp.concatenate(
        [mix_top, mix_low, mix_top, jnp.zeros((3, embed), jnp.float32), top, low, top]
        + [jnp.zeros((WIDE - at - 3 * extra, embed), jnp.float32)],
        axis=0,
    ).astype(jnp.bfloat16)
    stores = [
        pltpu.make_async_copy(src, dst, store_sem.at[i])
        for i, (src, dst) in enumerate(((first, first_out), (rest, rest_out), (second, second_out)))
    ]
    for copy in stores:
        copy.start()

    count = lon_dev // 2
    room = rows_f32.shape[1]
    for side in range(WIDE // LANES):
        rows_f32[side, count * GROUP :, :] = jnp.zeros((room - count * GROUP, LANES), jnp.float32)

    def finish_part(k):
        for copy in parts(k):
            copy.wait()
        v = [own[k, i] + incoming[0, k, i] + incoming[1, k, i] for i in range(GROUP - 1)]
        lane = lax.broadcasted_iota(jnp.int32, v[0].shape, 1)
        fields_of = [v[0]]
        for q in range(1, GROUP):
            both = v[q - 1] if q == GROUP - 1 else jnp.where(lane >= turns[q], v[q - 1], v[q])
            fields_of.append(pltpu.roll(both, LANES - turns[q], 1))
        for q in range(GROUP):
            top, low = halves(fields_of[q])
            flat = jnp.concatenate(
                [top, top, low, jnp.ones((3, LANES), jnp.float32)]
                + [jnp.zeros((WIDE - at, LANES), jnp.float32)],
                axis=0,
            )
            turned = flat.T[:count]
            for side in range(WIDE // LANES):
                rows_f32[side, pl.ds(q, count, stride=GROUP), :] = turned[
                    :, side * LANES : (side + 1) * LANES
                ]
        return jnp.concatenate([rows_f32[side] for side in range(WIDE // LANES)], axis=1).astype(
            jnp.bfloat16
        )

    def early_piece(k, carry):
        left[...] = finish_part(k)
        total = mlp_rows(fields, extra, left[...], first, rest, second, held)()
        result[...] = total[: count * GROUP].reshape(count, GROUP, embed)
        copy = pltpu.make_async_copy(result, early_out.at[k], result_sem)
        copy.start()
        copy.wait()
        return carry

    if early:
        lax.fori_loop(0, early, early_piece, 0)
    for k in range(early, pieces):
        left_out[k - early] = finish_part(k)
    for copy in stores:
        copy.wait()


def mlp(
    fields,
    extra,
    early,
    left_ref,
    first,
    rest,
    second_hbm,
    early_in,
    out,
    second,
    held,
    result,
    passing,
    load_sem,
    pass_in_sem,
    pass_out_sem,
    result_sem,
):
    late = left_ref.shape[0]
    count = result.shape[0]
    embed = result.shape[2]
    load = pltpu.make_async_copy(second_hbm, second, load_sem)
    load.start()
    place = lambda k: out.at[k // 2, pl.ds(k % 2 * count, count)]
    inward = [
        pltpu.make_async_copy(early_in.at[k], passing.at[k], pass_in_sem.at[k]) for k in range(early)
    ]
    outward = [
        pltpu.make_async_copy(passing.at[k], place(k), pass_out_sem.at[k]) for k in range(early)
    ]
    for copy in inward:
        copy.start()
    for i in range(late):
        k = early + i
        finish = mlp_rows(fields, extra, left_ref[i], first, rest, second, held)
        if i == 0:
            load.wait()
            for come, go in zip(inward, outward):
                come.wait()
                go.start()
        result[...] = finish()[: count * GROUP].reshape(count, GROUP, embed)
        copy = pltpu.make_async_copy(result, place(k), result_sem)
        copy.start()
        copy.wait()
    for copy in outward:
        copy.wait()


def per_device_fast(bands, columns, state, kernels, kernel_index, w_mix, w_in, b_in, w_out):
    members, lat_dev, fields, lon_dev = state.shape
    lat_half = lat_dev // 2
    pieces = 2 * members
    early = min(EARLY, pieces - 1)
    late = pieces - early
    count = lon_dev // 2
    embed, ffn = w_in.shape
    main = ffn // WIDE * WIDE
    depth = 3 * main + WIDE
    room = room_of(lon_dev)
    vmem = pl.BlockSpec(memory_space=pltpu.VMEM)
    hbm = pl.BlockSpec(memory_space=pl.ANY)
    f32 = jnp.float32
    half = jnp.bfloat16
    dma = pltpu.SemaphoreType.DMA
    packed = (pieces, GROUP - 1, fields, LANES)
    left, first, rest, second, ready = pl.pallas_call(
        functools.partial(exchange, bands, columns, early),
        out_shape=(
            jax.ShapeDtypeStruct((late, room, WIDE), half),
            jax.ShapeDtypeStruct((WIDE, main), half),
            jax.ShapeDtypeStruct((WIDE, WIDE), half),
            jax.ShapeDtypeStruct((depth, embed), half),
            jax.ShapeDtypeStruct((early, count, GROUP, embed), f32),
        ),
        in_specs=[pl.BlockSpec(memory_space=pltpu.SMEM)] + [vmem] * 3 + [hbm] * 3,
        out_specs=(vmem,) + (hbm,) * 4,
        scratch_shapes=[
            pltpu.VMEM(state.shape, f32),
            pltpu.VMEM(w_in.shape, f32),
            pltpu.VMEM(w_out.shape[::-1], f32),
            pltpu.VMEM((WIDE, main), half),
            pltpu.VMEM((WIDE, WIDE), half),
            pltpu.VMEM((depth, embed), half),
            pltpu.VMEM((room, WIDE), half),
            pltpu.VMEM((WIDE // LANES, room, LANES), f32),
            pltpu.VMEM((room, depth), half),
            pltpu.VMEM((count, GROUP, embed), f32),
            pltpu.VMEM(state.shape, f32),
            pltpu.VMEM((2, members, fields, lon_dev), f32),
            pltpu.VMEM((members, lat_dev + 1, 4, fields, LANES), f32),
            pltpu.VMEM((lat_half * 3, 2 * TAPS - 3, fields, LANES), f32),
            pltpu.VMEM(packed, f32),
            pltpu.VMEM((2,) + packed, f32),
            pltpu.VMEM((2,) + packed, f32),
            dma((members + 2,)),
            dma((3,)),
            dma(()),
            dma((members,)),
            dma((members,)),
            dma((2, members)),
            dma((2, members)),
            dma((2, pieces)),
            dma((2, pieces)),
        ],
        compiler_params=pltpu.CompilerParams(
            collective_id=0, has_side_effects=True, vmem_limit_bytes=60 * 2**20
        ),
        name="exchange",
    )(
        kernel_index,
        jnp.transpose(kernels, (0, 2, 1, 3)),
        w_mix,
        b_in,
        state,
        w_in,
        w_out.T,
    )
    out = pl.pallas_call(
        functools.partial(mlp, fields, ffn - main, early),
        out_shape=jax.ShapeDtypeStruct((members, lon_dev, lat_half, embed), f32),
        in_specs=[vmem] * 3 + [hbm] * 2,
        out_specs=hbm,
        scratch_shapes=[
            pltpu.VMEM((depth, embed), half),
            pltpu.VMEM((room, depth), half),
            pltpu.VMEM((count, GROUP, embed), f32),
            pltpu.VMEM((early, count, GROUP, embed), f32),
            dma(()),
            dma((early,)),
            dma((early,)),
            dma(()),
        ],
        compiler_params=pltpu.CompilerParams(vmem_limit_bytes=56 * 2**20),
        name="mlp",
    )(left, first, rest, second, ready)
    return jnp.transpose(out, (0, 2, 1, 3))


def fits(mesh, state, w_in):
    bands, columns = mesh.shape["polar"], mesh.shape["azimuth"]
    members, lat, fields, lon = state.shape
    main = w_in.shape[1] // WIDE * WIDE
    return (
        bands >= 2
        and columns % 2 == 0
        and columns >= 6
        and lon == 2 * SPACING * columns
        and lat == 2 * GROUP * bands
        and fields % SUB == 0
        and main > 0
        and 3 * fields + 3 + 3 * (w_in.shape[1] - main) <= WIDE
    )


def solution(mesh):
    placed = (P(None, "polar", None, "azimuth"), P(), P(), P(), P(), P(), P())

    def run(state, kernels, kernel_index, w_mix, w_in, b_in, w_out):
        body = per_device
        if fits(mesh, state, w_in):
            body = functools.partial(per_device_fast, mesh.shape["polar"], mesh.shape["azimuth"])
        return jax.shard_map(
            body,
            mesh=mesh,
            in_specs=placed,
            out_specs=P(None, "polar", "azimuth", None),
            check_vma=False,
        )(state, kernels, kernel_index, w_mix, w_in, b_in, w_out)

    return run
```

```python
import functools

import jax
import jax.numpy as jnp
from jax import lax
from jax.experimental import pallas as pl
from jax.experimental.pallas import tpu as pltpu
from jax.sharding import PartitionSpec as P

TAPS = 9
SPACING = 90


def shifted(array, axis, by):
    peers = lax.axis_size(axis)
    pairs = [(i, i + by) for i in range(peers) if 0 <= i + by < peers]
    return lax.ppermute(array, axis, pairs)


def row_taps(kernels, kernel_index, out_lat, tap_pos, channel, valid):
    fields = kernels.shape[3]
    total_out = kernel_index.shape[0]
    pick = (out_lat[:, None] == jnp.arange(total_out, dtype=jnp.int32)[None, :]).astype(jnp.int32)
    kernel_of = jnp.sum(pick * kernel_index[None, :], axis=1)
    one_kernel = (
        kernel_of[:, None] == jnp.arange(kernels.shape[0], dtype=jnp.int32)[None, :]
    ).astype(jnp.float32)
    one_tap = (tap_pos[:, None] == jnp.arange(3, dtype=jnp.int32)[None, :]).astype(jnp.float32)
    one_field = (channel[:, None] == jnp.arange(fields, dtype=jnp.int32)[None, :]).astype(
        jnp.float32
    )
    chosen = jnp.einsum(
        "rk,ra,rc,katc->rt",
        one_kernel,
        one_tap,
        one_field,
        kernels,
        precision=lax.Precision.HIGHEST,
        preferred_element_type=jnp.float32,
    )
    return chosen * valid[:, None]


def correlate(cycle, weights):
    half = TAPS // 2
    total = jnp.zeros(cycle.shape, jnp.float32)
    for tap in range(TAPS):
        total = total + weights[:, tap : tap + 1] * jnp.roll(cycle, -(tap - half) * SPACING, axis=1)
    return total


def finish(summed, w_mix, w_in, b_in, w_out):
    lat_half, fields, lon_dev = summed.shape
    mixed = jnp.einsum(
        "ocl,ce->ole",
        summed,
        w_mix,
        precision=lax.Precision.HIGHEST,
        preferred_element_type=jnp.float32,
    ).reshape(lat_half * lon_dev, -1)
    pre = (
        jnp.dot(mixed, w_in, precision=lax.Precision.HIGHEST, preferred_element_type=jnp.float32)
        + b_in
    )
    hidden = jax.nn.gelu(pre, approximate=False)
    out = mixed + jnp.dot(
        hidden, w_out, precision=lax.Precision.HIGHEST, preferred_element_type=jnp.float32
    )
    return out.reshape(lat_half, lon_dev, -1)


def per_device(state, kernels, kernel_index, w_mix, w_in, b_in, w_out):
    members, lat_dev, fields, lon_dev = state.shape
    lat_half = lat_dev // 2
    azim = lax.axis_index("azimuth")
    band = lax.axis_index("polar")
    total_out = kernel_index.shape[0]
    results = []
    for member in range(members):
        block = state[member]
        flat = block.reshape(lat_dev * fields, lon_dev)
        cycle = lax.all_to_all(flat, "azimuth", split_axis=0, concat_axis=1, tiled=True)
        rows_here = cycle.shape[0]
        index = azim * rows_here + jnp.arange(rows_here, dtype=jnp.int32)
        glob = band * lat_dev + index // fields
        channel = index % fields
        parity = glob % 2
        first_w = row_taps(
            kernels,
            kernel_index,
            glob // 2,
            1 + parity,
            channel,
            jnp.ones((rows_here,), jnp.float32),
        )
        second_out = (glob + 1) // 2
        second_ok = ((parity == 1) & (second_out < total_out)).astype(jnp.float32)
        second_w = row_taps(
            kernels, kernel_index, second_out, jnp.zeros_like(glob), channel, second_ok
        )
        planes = jnp.stack([correlate(cycle, first_w), correlate(cycle, second_w)])
        back = lax.all_to_all(planes, "azimuth", split_axis=2, concat_axis=1, tiled=True)
        back = back.reshape(2, lat_half, 2, fields, lon_dev)
        near = back[0, :, 0] + back[0, :, 1]
        upper = back[1, :, 1]
        edge = shifted(upper[-1], "polar", 1)
        summed = near + jnp.concatenate([edge[None], upper[:-1]], axis=0)
        results.append(finish(summed, w_mix, w_in, b_in, w_out))
    return jnp.stack(results)


LANES = 128
SUB = 8
GROUP = 4
WIDE = 256
MESH = pl.DeviceIdType.MESH


def halves(x):
    top = x.astype(jnp.bfloat16).astype(jnp.float32)
    return top, x - top


def room_of(lon_dev):
    return -(-(lon_dev // 2 * GROUP) // 16) * 16


def mlp_rows(fields, extra, left16, first, rest, second, held):
    main = first.shape[1]
    at = 3 * fields + 3
    low_at = at + 2 * extra

    def act(weights):
        pre = jnp.dot(left16, weights, preferred_element_type=jnp.float32)
        return pre * 0.5 * (1.0 + lax.erf(pre * (0.5**0.5)))

    for c in range(main // WIDE):
        hidden = act(first[:, c * WIDE : (c + 1) * WIDE])
        top = hidden.astype(jnp.bfloat16)
        low = (hidden - top.astype(jnp.float32)).astype(jnp.bfloat16)
        held[:, c * WIDE : (c + 1) * WIDE] = top
        held[:, main + c * WIDE : main + (c + 1) * WIDE] = top
        held[:, 2 * main + c * WIDE : 2 * main + (c + 1) * WIDE] = low
    top, low = halves(act(rest[...]))
    lane = lax.broadcasted_iota(jnp.int32, top.shape, 1)
    mixed = jnp.where(
        lane < at,
        left16.astype(jnp.float32),
        jnp.where(lane < low_at, top, jnp.where(lane < low_at + extra, low, 0.0)),
    )
    held[:, 3 * main :] = mixed.astype(jnp.bfloat16)
    return lambda: jnp.dot(held[...], second[...], preferred_element_type=jnp.float32)


def exchange(
    bands,
    columns,
    idx_ref,
    kern,
    w_mix,
    b_in,
    st_hbm,
    w_in_hbm,
    w_out_hbm,
    early_out,
    st,
    w_in,
    w_out,
    first,
    rest,
    second,
    left,
    rows_f32,
    held,
    result,
    peer,
    edge,
    blocks,
    taps,
    own,
    outgoing,
    incoming,
    load_sem,
    result_sem,
    peer_send,
    peer_recv,
    edge_send,
    edge_recv,
    relay_send,
    relay_recv,
    part_send,
    part_recv,
):
    members, lat_dev, fields, lon_dev = st.shape
    lat_half = lat_dev // 2
    tiles = fields // SUB
    embed, ffn = w_in.shape
    pieces = 2 * members
    az = lax.axis_index("azimuth")
    band = lax.axis_index("polar")
    core = lax.rem(az, 2)
    chip = az // 2
    chips = columns // 2
    mate = chip * 2 + 1 - core
    up = lax.rem(chip + 1, chips) * 2 + core
    down = lax.rem(chip + chips - 1, chips) * 2 + core
    next_band = lax.rem(band + 1, bands)
    last_band = lax.rem(band + bands - 1, bands)

    loads = [pltpu.make_async_copy(st_hbm.at[m], st.at[m], load_sem.at[m]) for m in range(members)]
    load_in = pltpu.make_async_copy(w_in_hbm, w_in, load_sem.at[members])
    load_out = pltpu.make_async_copy(w_out_hbm, w_out, load_sem.at[members + 1])
    for copy in loads:
        copy.start()

    barrier = pltpu.get_barrier_semaphore()
    for who in ((band, mate), (band, up), (band, down), (last_band, az)):
        pl.semaphore_signal(barrier, inc=1, device_id=who, device_id_type=MESH)
    pl.semaphore_wait(barrier, 4)

    def remote(src, dst, send, recv, who):
        return pltpu.make_async_remote_copy(
            src_ref=src, dst_ref=dst, send_sem=send, recv_sem=recv, device_id=who, device_id_type=MESH
        )

    peers = []
    edges = []
    relays = []
    for m in range(members):
        peers.append(remote(st_hbm.at[m], peer.at[m], peer_send.at[m], peer_recv.at[m], (band, mate)))
        edges.append(
            remote(
                st_hbm.at[m, lat_dev - 1], edge.at[0, m], edge_send.at[m], edge_recv.at[m], (next_band, az)
            )
        )
        relays.append(
            remote(edge.at[0, m], edge.at[1, m], relay_send.at[m], relay_recv.at[m], (band, mate))
        )
    for m in range(members):
        edges[m].start()
        peers[m].start()
    load_in.start()
    load_out.start()

    half = TAPS // 2
    pad = half - 1
    for o in range(lat_half):
        k = idx_ref[band * lat_half + o]
        for a in range(3):
            columns_of = kern[k, :, a, :].T
            if o == 0 and a == 0:
                columns_of = columns_of * jnp.where(band > 0, 1.0, 0.0)
            for t in range(TAPS):
                taps[o * 3 + a, t + pad] = jnp.broadcast_to(columns_of[:, t : t + 1], (fields, LANES))
            for t in range(pad):
                taps[o * 3 + a, t] = jnp.zeros((fields, LANES), jnp.float32)
                taps[o * 3 + a, t + pad + TAPS] = jnp.zeros((fields, LANES), jnp.float32)

    spare = lon_dev - LANES

    def unpack(src, m, lat, to):
        x = src[:, :LANES]
        y = src[:, LANES:]
        y = jnp.concatenate([y, jnp.zeros((fields, LANES - spare), jnp.float32)], axis=1)
        lane = lax.broadcasted_iota(jnp.int32, x.shape, 1)
        blocks[m, lat, to] = x
        blocks[m, lat, to + 1] = pltpu.roll(jnp.where(lane < SPACING, y, x), LANES - SPACING, 1)

    turns = [q * SPACING % LANES for q in range(GROUP)]

    def pack(value, ref, at, rows):
        lane = lax.broadcasted_iota(jnp.int32, (SUB, LANES), 1)
        turned = [value[0]] + [pltpu.roll(value[q], turns[q], 1) for q in range(1, GROUP)]
        ref[at + (0, rows, slice(None))] = jnp.where(lane < turns[1], turned[0], turned[1])
        ref[at + (1, rows, slice(None))] = jnp.where(lane < turns[2], turned[1], turned[2])
        ref[at + (2, rows, slice(None))] = jnp.where(lane < turns[3], turned[2], turned[3])

    def correlate_member(m):
        def body(r, carry):
            rows = pl.ds(pl.multiple_of(r * SUB, SUB), SUB)
            total = [[[None] * lat_half for _ in range(2)] for _ in range(3)]
            for o in range(lat_half):
                for a in range(3):
                    x = [blocks[m, 2 * o + a, b, rows, :] for b in range(4)]
                    for target in range(3):
                        base = pad + half * target - 2 * core
                        w = {d: taps[o * 3 + a, base + d, rows, :] for d in range(-1, 4)}
                        for j in range(2):
                            term = w[-j] * x[0]
                            for b in range(1, 4):
                                term = term + w[b - j] * x[b]
                            old = total[target][j][o]
                            total[target][j][o] = term if old is None else old + term
            for j in range(2):
                pack(total[0][j], outgoing, (0, 2 * m + j), rows)
                pack(total[1][j], own, (2 * m + j,), rows)
                pack(total[2][j], outgoing, (1, 2 * m + j), rows)
            return carry

        lax.fori_loop(0, tiles, body, 0)

    def parts(k):
        return [
            remote(
                outgoing.at[way, k],
                incoming.at[way, k],
                part_send.at[way, k],
                part_recv.at[way, k],
                (band, who),
            )
            for way, who in enumerate((up, down))
        ]

    mine = 2 * core
    theirs = 2 - 2 * core
    for m in range(members):
        edges[m].wait()
        relays[m].start()
        loads[m].wait()
        for lat in range(lat_dev):
            unpack(st.at[m, lat], m, lat + 1, mine)
        unpack(edge.at[0, m], m, 0, mine)
        peers[m].wait()
        for lat in range(lat_dev):
            unpack(peer.at[m, lat], m, lat + 1, theirs)
        relays[m].wait()
        unpack(edge.at[1, m], m, 0, theirs)
        correlate_member(m)
        for j in range(2):
            for copy in parts(2 * m + j):
                copy.start()

    main = ffn // WIDE * WIDE
    extra = ffn - main
    at = 3 * fields + 3
    mix_top, mix_low = halves(w_mix[...])
    stacked = jnp.concatenate([mix_top, mix_low], axis=0).astype(jnp.bfloat16)
    load_in.wait()

    def product(cols):
        in_top, in_low = halves(w_in[:, cols])
        big = jnp.dot(stacked, in_top.astype(jnp.bfloat16), preferred_element_type=jnp.float32)
        small = jnp.dot(
            mix_top.astype(jnp.bfloat16), in_low.astype(jnp.bfloat16), preferred_element_type=jnp.float32
        )
        whole = big[:fields] + (big[fields:] + small)
        top, low = halves(whole)
        bias, leave = halves(b_in[cols][None, :])
        bias_low, leave = halves(leave)
        width = whole.shape[1]
        return jnp.concatenate(
            [top, low, top, bias, bias_low, leave, jnp.zeros((WIDE - at, width), jnp.float32)], axis=0
        )

    for c in range(main // WIDE):
        cols = slice(c * WIDE, (c + 1) * WIDE)
        first[:, cols] = product(cols).astype(jnp.bfloat16)
    tail = product(slice(main, ffn))
    rest[...] = jnp.concatenate(
        [jnp.zeros((WIDE, at), jnp.float32)]
        + [tail] * 3
        + [jnp.zeros((WIDE, WIDE - at - 3 * extra), jnp.float32)],
        axis=1,
    ).astype(jnp.bfloat16)
    load_out.wait()
    for c in range(main // WIDE):
        top, low = halves(w_out[:, c * WIDE : (c + 1) * WIDE].T)
        base = c * WIDE
        second[base : base + WIDE, :] = top.astype(jnp.bfloat16)
        second[base + main : base + main + WIDE, :] = low.astype(jnp.bfloat16)
        second[base + 2 * main : base + 2 * main + WIDE, :] = top.astype(jnp.bfloat16)
    top, low = halves(w_out[:, main:].T)
    second[3 * main :, :] = jnp.concatenate(
        [mix_top, mix_low, mix_top, jnp.zeros((3, embed), jnp.float32), top, low, top]
        + [jnp.zeros((WIDE - at - 3 * extra, embed), jnp.float32)],
        axis=0,
    ).astype(jnp.bfloat16)

    count = lon_dev // 2
    room = rows_f32.shape[1]
    for side in range(WIDE // LANES):
        rows_f32[side, count * GROUP :, :] = jnp.zeros((room - count * GROUP, LANES), jnp.float32)

    def finish_part(k):
        for copy in parts(k):
            copy.wait()
        v = [own[k, i] + incoming[0, k, i] + incoming[1, k, i] for i in range(GROUP - 1)]
        lane = lax.broadcasted_iota(jnp.int32, v[0].shape, 1)
        fields_of = [v[0]]
        for q in range(1, GROUP):
            both = v[q - 1] if q == GROUP - 1 else jnp.where(lane >= turns[q], v[q - 1], v[q])
            fields_of.append(pltpu.roll(both, LANES - turns[q], 1))
        for q in range(GROUP):
            top, low = halves(fields_of[q])
            flat = jnp.concatenate(
                [top, top, low, jnp.ones((3, LANES), jnp.float32)]
                + [jnp.zeros((WIDE - at, LANES), jnp.float32)],
                axis=0,
            )
            turned = flat.T[:count]
            for side in range(WIDE // LANES):
                rows_f32[side, pl.ds(q, count, stride=GROUP), :] = turned[
                    :, side * LANES : (side + 1) * LANES
                ]
        return jnp.concatenate([rows_f32[side] for side in range(WIDE // LANES)], axis=1).astype(
            jnp.bfloat16
        )

    def store_of(k):
        return pltpu.make_async_copy(result, early_out.at[k], result_sem)

    def piece(k, carry):
        left[...] = finish_part(k)
        total = mlp_rows(fields, extra, left[...], first, rest, second, held)()

        @pl.when(k > 0)
        def _():
            store_of(k - 1).wait()

        result[...] = total[: count * GROUP].reshape(count, GROUP, embed)
        store_of(k).start()
        return carry

    lax.fori_loop(0, pieces, piece, 0)
    store_of(pieces - 1).wait()


def deliver(made, out, passing, in_sem, out_sem):
    pieces, count = made.shape[:2]
    inward = [pltpu.make_async_copy(made.at[k], passing.at[k], in_sem.at[k]) for k in range(pieces)]
    outward = [
        pltpu.make_async_copy(
            passing.at[k], out.at[k // 2, pl.ds(k % 2 * count, count)], out_sem.at[k]
        )
        for k in range(pieces)
    ]
    for copy in inward:
        copy.start()
    for come, go in zip(inward, outward):
        come.wait()
        go.start()
    for copy in outward:
        copy.wait()


def per_device_fast(bands, columns, state, kernels, kernel_index, w_mix, w_in, b_in, w_out):
    members, lat_dev, fields, lon_dev = state.shape
    lat_half = lat_dev // 2
    pieces = 2 * members
    count = lon_dev // 2
    embed, ffn = w_in.shape
    main = ffn // WIDE * WIDE
    depth = 3 * main + WIDE
    room = room_of(lon_dev)
    vmem = pl.BlockSpec(memory_space=pltpu.VMEM)
    hbm = pl.BlockSpec(memory_space=pl.ANY)
    f32 = jnp.float32
    half = jnp.bfloat16
    dma = pltpu.SemaphoreType.DMA
    packed = (pieces, GROUP - 1, fields, LANES)
    made = pl.pallas_call(
        functools.partial(exchange, bands, columns),
        out_shape=jax.ShapeDtypeStruct((pieces, count, GROUP, embed), f32),
        in_specs=[pl.BlockSpec(memory_space=pltpu.SMEM)] + [vmem] * 3 + [hbm] * 3,
        out_specs=hbm,
        scratch_shapes=[
            pltpu.VMEM(state.shape, f32),
            pltpu.VMEM(w_in.shape, f32),
            pltpu.VMEM(w_out.shape[::-1], f32),
            pltpu.VMEM((WIDE, main), half),
            pltpu.VMEM((WIDE, WIDE), half),
            pltpu.VMEM((depth, embed), half),
            pltpu.VMEM((room, WIDE), half),
            pltpu.VMEM((WIDE // LANES, room, LANES), f32),
            pltpu.VMEM((room, depth), half),
            pltpu.VMEM((count, GROUP, embed), f32),
            pltpu.VMEM(state.shape, f32),
            pltpu.VMEM((2, members, fields, lon_dev), f32),
            pltpu.VMEM((members, lat_dev + 1, 4, fields, LANES), f32),
            pltpu.VMEM((lat_half * 3, 2 * TAPS - 3, fields, LANES), f32),
            pltpu.VMEM(packed, f32),
            pltpu.VMEM((2,) + packed, f32),
            pltpu.VMEM((2,) + packed, f32),
            dma((members + 2,)),
            dma(()),
            dma((members,)),
            dma((members,)),
            dma((members,)),
            dma((members,)),
            dma((members,)),
            dma((members,)),
            dma((2, pieces)),
            dma((2, pieces)),
        ],
        compiler_params=pltpu.CompilerParams(
            collective_id=0, has_side_effects=True, vmem_limit_bytes=60 * 2**20
        ),
        name="exchange",
    )(
        kernel_index,
        jnp.transpose(kernels, (0, 2, 1, 3)),
        w_mix,
        b_in,
        state,
        w_in,
        w_out.T,
    )
    out = pl.pallas_call(
        deliver,
        out_shape=jax.ShapeDtypeStruct((members, lon_dev, lat_half, embed), f32),
        in_specs=[hbm],
        out_specs=hbm,
        scratch_shapes=[
            pltpu.VMEM((pieces, count, GROUP, embed), f32),
            dma((pieces,)),
            dma((pieces,)),
        ],
        compiler_params=pltpu.CompilerParams(vmem_limit_bytes=32 * 2**20),
        name="deliver",
    )(made)
    return jnp.transpose(out, (0, 2, 1, 3))


def fits(mesh, state, w_in):
    bands, columns = mesh.shape["polar"], mesh.shape["azimuth"]
    members, lat, fields, lon = state.shape
    main = w_in.shape[1] // WIDE * WIDE
    return (
        bands >= 2
        and columns % 2 == 0
        and columns >= 6
        and lon == 2 * SPACING * columns
        and lat == 2 * GROUP * bands
        and fields % SUB == 0
        and main > 0
        and 3 * fields + 3 + 3 * (w_in.shape[1] - main) <= WIDE
    )


def solution(mesh):
    placed = (P(None, "polar", None, "azimuth"), P(), P(), P(), P(), P(), P())

    def run(state, kernels, kernel_index, w_mix, w_in, b_in, w_out):
        body = per_device
        if fits(mesh, state, w_in):
            body = functools.partial(per_device_fast, mesh.shape["polar"], mesh.shape["azimuth"])
        return jax.shard_map(
            body,
            mesh=mesh,
            in_specs=placed,
            out_specs=P(None, "polar", "azimuth", None),
            check_vma=False,
        )(state, kernels, kernel_index, w_mix, w_in, b_in, w_out)

    return run
```

```python
import functools
import math

import jax
import jax.numpy as jnp
from jax import lax
from jax.experimental import pallas as pl
from jax.experimental.pallas import tpu as pltpu
from jax.sharding import PartitionSpec as P

TAPS = 9
SPACING = 90


def shifted(array, axis, by):
    peers = lax.axis_size(axis)
    pairs = [(i, i + by) for i in range(peers) if 0 <= i + by < peers]
    return lax.ppermute(array, axis, pairs)


def row_taps(kernels, kernel_index, out_lat, tap_pos, channel, valid):
    fields = kernels.shape[3]
    total_out = kernel_index.shape[0]
    pick = (out_lat[:, None] == jnp.arange(total_out, dtype=jnp.int32)[None, :]).astype(jnp.int32)
    kernel_of = jnp.sum(pick * kernel_index[None, :], axis=1)
    one_kernel = (
        kernel_of[:, None] == jnp.arange(kernels.shape[0], dtype=jnp.int32)[None, :]
    ).astype(jnp.float32)
    one_tap = (tap_pos[:, None] == jnp.arange(3, dtype=jnp.int32)[None, :]).astype(jnp.float32)
    one_field = (channel[:, None] == jnp.arange(fields, dtype=jnp.int32)[None, :]).astype(
        jnp.float32
    )
    chosen = jnp.einsum(
        "rk,ra,rc,katc->rt",
        one_kernel,
        one_tap,
        one_field,
        kernels,
        precision=lax.Precision.HIGHEST,
        preferred_element_type=jnp.float32,
    )
    return chosen * valid[:, None]


def correlate(cycle, weights):
    half = TAPS // 2
    total = jnp.zeros(cycle.shape, jnp.float32)
    for tap in range(TAPS):
        total = total + weights[:, tap : tap + 1] * jnp.roll(cycle, -(tap - half) * SPACING, axis=1)
    return total


def finish(summed, w_mix, w_in, b_in, w_out):
    lat_half, fields, lon_dev = summed.shape
    mixed = jnp.einsum(
        "ocl,ce->ole",
        summed,
        w_mix,
        precision=lax.Precision.HIGHEST,
        preferred_element_type=jnp.float32,
    ).reshape(lat_half * lon_dev, -1)
    pre = (
        jnp.dot(mixed, w_in, precision=lax.Precision.HIGHEST, preferred_element_type=jnp.float32)
        + b_in
    )
    hidden = jax.nn.gelu(pre, approximate=False)
    out = mixed + jnp.dot(
        hidden, w_out, precision=lax.Precision.HIGHEST, preferred_element_type=jnp.float32
    )
    return out.reshape(lat_half, lon_dev, -1)


def per_device(state, kernels, kernel_index, w_mix, w_in, b_in, w_out):
    members, lat_dev, fields, lon_dev = state.shape
    lat_half = lat_dev // 2
    azim = lax.axis_index("azimuth")
    band = lax.axis_index("polar")
    total_out = kernel_index.shape[0]
    results = []
    for member in range(members):
        block = state[member]
        flat = block.reshape(lat_dev * fields, lon_dev)
        cycle = lax.all_to_all(flat, "azimuth", split_axis=0, concat_axis=1, tiled=True)
        rows_here = cycle.shape[0]
        index = azim * rows_here + jnp.arange(rows_here, dtype=jnp.int32)
        glob = band * lat_dev + index // fields
        channel = index % fields
        parity = glob % 2
        first_w = row_taps(
            kernels,
            kernel_index,
            glob // 2,
            1 + parity,
            channel,
            jnp.ones((rows_here,), jnp.float32),
        )
        second_out = (glob + 1) // 2
        second_ok = ((parity == 1) & (second_out < total_out)).astype(jnp.float32)
        second_w = row_taps(
            kernels, kernel_index, second_out, jnp.zeros_like(glob), channel, second_ok
        )
        planes = jnp.stack([correlate(cycle, first_w), correlate(cycle, second_w)])
        back = lax.all_to_all(planes, "azimuth", split_axis=2, concat_axis=1, tiled=True)
        back = back.reshape(2, lat_half, 2, fields, lon_dev)
        near = back[0, :, 0] + back[0, :, 1]
        upper = back[1, :, 1]
        edge = shifted(upper[-1], "polar", 1)
        summed = near + jnp.concatenate([edge[None], upper[:-1]], axis=0)
        results.append(finish(summed, w_mix, w_in, b_in, w_out))
    return jnp.stack(results)


LANES = 128
SUB = 8
GROUP = 4
WIDE = 256
MESH = pl.DeviceIdType.MESH


def halves(x):
    top = x.astype(jnp.bfloat16).astype(jnp.float32)
    return top, x - top


def room_of(lon_dev):
    return -(-(lon_dev // 2 * GROUP) // 16) * 16


ERFC = (0.254829592, -0.284496736, 1.421413741, -1.453152027, 1.061405429)
ERFC_P = 0.3275911


def gelu(x):
    size = jnp.abs(x)
    base = size * (ERFC_P * 0.5**0.5) + 1.0
    guess = pl.reciprocal(base, approx=True)
    t = guess * (2.0 - base * guess)
    poly = ERFC[4] * 0.5
    for coefficient in ERFC[3::-1]:
        poly = poly * t + coefficient * 0.5
    upper = poly * t * jnp.exp2(x * x * (-0.5 / math.log(2.0)))
    return jnp.maximum(x, 0.0) - size * upper


def mlp_rows(fields, extra, left16, first, rest, second, held):
    chunks = first.shape[1] // WIDE
    at = 3 * fields + 3
    low_at = at + 2 * extra

    def act(weights):
        return gelu(jnp.dot(left16, weights, preferred_element_type=jnp.float32))

    total = None
    done = 0
    for c in range(chunks):
        hidden = act(first[:, c * WIDE : (c + 1) * WIDE])
        top = hidden.astype(jnp.bfloat16)
        low = (hidden - top.astype(jnp.float32)).astype(jnp.bfloat16)
        base = 3 * c * WIDE
        held[:, base : base + WIDE] = top
        held[:, base + WIDE : base + 2 * WIDE] = top
        held[:, base + 2 * WIDE : base + 3 * WIDE] = low
        if c == chunks - 1:
            top, low = halves(act(rest[...]))
            lane = lax.broadcasted_iota(jnp.int32, top.shape, 1)
            mixed = jnp.where(
                lane < at,
                left16.astype(jnp.float32),
                jnp.where(lane < low_at, top, jnp.where(lane < low_at + extra, low, 0.0)),
            )
            held[:, 3 * chunks * WIDE :] = mixed.astype(jnp.bfloat16)
        if c % 2 == 1 or c == chunks - 1:
            upto = base + 3 * WIDE if c < chunks - 1 else held.shape[1]
            term = jnp.dot(held[:, done:upto], second[done:upto, :], preferred_element_type=jnp.float32)
            total = term if total is None else total + term
            done = upto
    return total


def exchange(
    bands,
    columns,
    idx_ref,
    kern,
    w_mix,
    b_in,
    st_hbm,
    w_in_hbm,
    w_out_hbm,
    early_out,
    st,
    w_in,
    w_out,
    first,
    rest,
    second,
    left,
    rows_f32,
    held,
    result,
    peer,
    edge,
    blocks,
    taps,
    own,
    outgoing,
    incoming,
    load_sem,
    result_sem,
    peer_send,
    peer_recv,
    edge_send,
    edge_recv,
    relay_send,
    relay_recv,
    part_send,
    part_recv,
):
    members, lat_dev, fields, lon_dev = st.shape
    lat_half = lat_dev // 2
    tiles = fields // SUB
    embed, ffn = w_in.shape
    pieces = 2 * members
    az = lax.axis_index("azimuth")
    band = lax.axis_index("polar")
    core = lax.rem(az, 2)
    chip = az // 2
    chips = columns // 2
    mate = chip * 2 + 1 - core
    up = lax.rem(chip + 1, chips) * 2 + core
    down = lax.rem(chip + chips - 1, chips) * 2 + core
    next_band = lax.rem(band + 1, bands)
    last_band = lax.rem(band + bands - 1, bands)

    loads = [pltpu.make_async_copy(st_hbm.at[m], st.at[m], load_sem.at[m]) for m in range(members)]
    load_in = pltpu.make_async_copy(w_in_hbm, w_in, load_sem.at[members])
    load_out = pltpu.make_async_copy(w_out_hbm, w_out, load_sem.at[members + 1])
    for copy in loads:
        copy.start()

    barrier = pltpu.get_barrier_semaphore()
    for who in ((band, mate), (band, up), (band, down), (last_band, az)):
        pl.semaphore_signal(barrier, inc=1, device_id=who, device_id_type=MESH)
    pl.semaphore_wait(barrier, 4)

    def remote(src, dst, send, recv, who):
        return pltpu.make_async_remote_copy(
            src_ref=src, dst_ref=dst, send_sem=send, recv_sem=recv, device_id=who, device_id_type=MESH
        )

    peers = []
    edges = []
    relays = []
    for m in range(members):
        peers.append(remote(st_hbm.at[m], peer.at[m], peer_send.at[m], peer_recv.at[m], (band, mate)))
        edges.append(
            remote(
                st_hbm.at[m, lat_dev - 1], edge.at[0, m], edge_send.at[m], edge_recv.at[m], (next_band, az)
            )
        )
        relays.append(
            remote(edge.at[0, m], edge.at[1, m], relay_send.at[m], relay_recv.at[m], (band, mate))
        )
    for m in range(members):
        edges[m].start()
        peers[m].start()
    load_in.start()
    load_out.start()

    half = TAPS // 2
    pad = half - 1
    for o in range(lat_half):
        k = idx_ref[band * lat_half + o]
        for a in range(3):
            columns_of = kern[k, :, a, :].T
            if o == 0 and a == 0:
                columns_of = columns_of * jnp.where(band > 0, 1.0, 0.0)
            for t in range(TAPS):
                taps[o * 3 + a, t + pad] = jnp.broadcast_to(columns_of[:, t : t + 1], (fields, LANES))
            for t in range(pad):
                taps[o * 3 + a, t] = jnp.zeros((fields, LANES), jnp.float32)
                taps[o * 3 + a, t + pad + TAPS] = jnp.zeros((fields, LANES), jnp.float32)

    spare = lon_dev - LANES

    def unpack(src, m, lat, to):
        x = src[:, :LANES]
        y = src[:, LANES:]
        y = jnp.concatenate([y, jnp.zeros((fields, LANES - spare), jnp.float32)], axis=1)
        lane = lax.broadcasted_iota(jnp.int32, x.shape, 1)
        blocks[m, lat, to] = x
        blocks[m, lat, to + 1] = pltpu.roll(jnp.where(lane < SPACING, y, x), LANES - SPACING, 1)

    turns = [q * SPACING % LANES for q in range(GROUP)]

    def pack(value, ref, at, rows):
        lane = lax.broadcasted_iota(jnp.int32, (SUB, LANES), 1)
        turned = [value[0]] + [pltpu.roll(value[q], turns[q], 1) for q in range(1, GROUP)]
        ref[at + (0, rows, slice(None))] = jnp.where(lane < turns[1], turned[0], turned[1])
        ref[at + (1, rows, slice(None))] = jnp.where(lane < turns[2], turned[1], turned[2])
        ref[at + (2, rows, slice(None))] = jnp.where(lane < turns[3], turned[2], turned[3])

    def correlate_member(m):
        def body(r, carry):
            rows = pl.ds(pl.multiple_of(r * SUB, SUB), SUB)
            total = [[[None] * lat_half for _ in range(2)] for _ in range(3)]
            for o in range(lat_half):
                for a in range(1 if o == 0 else 0, 3):
                    x = [blocks[m, 2 * o + a, b, rows, :] for b in range(4)]
                    for target in range(3):
                        base = pad + half * target - 2 * core
                        w = {d: taps[o * 3 + a, base + d, rows, :] for d in range(-1, 4)}
                        for j in range(2):
                            term = w[-j] * x[0]
                            for b in range(1, 4):
                                term = term + w[b - j] * x[b]
                            old = total[target][j][o]
                            total[target][j][o] = term if old is None else old + term
            for j in range(2):
                pack(total[0][j], outgoing, (0, 2 * m + j), rows)
                pack(total[1][j], own, (2 * m + j,), rows)
                pack(total[2][j], outgoing, (1, 2 * m + j), rows)
            return carry

        lax.fori_loop(0, tiles, body, 0)

    def add_edge(m):
        def body(r, carry):
            rows = pl.ds(pl.multiple_of(r * SUB, SUB), SUB)
            lane = lax.broadcasted_iota(jnp.int32, (SUB, LANES), 1)
            x = [blocks[m, 0, b, rows, :] for b in range(4)]
            for target in range(3):
                base = pad + half * target - 2 * core
                w = {d: taps[0, base + d, rows, :] for d in range(-1, 4)}
                for j in range(2):
                    term = w[-j] * x[0]
                    for b in range(1, 4):
                        term = term + w[b - j] * x[b]
                    ref = own if target == 1 else outgoing.at[target // 2]
                    old = ref[2 * m + j, 0, rows, :]
                    ref[2 * m + j, 0, rows, :] = old + jnp.where(lane < SPACING, term, 0.0)
            return carry

        lax.fori_loop(0, tiles, body, 0)

    def parts(k):
        return [
            remote(
                outgoing.at[way, k],
                incoming.at[way, k],
                part_send.at[way, k],
                part_recv.at[way, k],
                (band, who),
            )
            for way, who in enumerate((up, down))
        ]

    mine = 2 * core
    theirs = 2 - 2 * core
    for m in range(members):
        loads[m].wait()
        for lat in range(lat_dev):
            unpack(st.at[m, lat], m, lat + 1, mine)
        if m == 0:
            edges[0].wait()
            relays[0].start()
        peers[m].wait()
        for lat in range(lat_dev):
            unpack(peer.at[m, lat], m, lat + 1, theirs)
        correlate_member(m)
        unpack(edge.at[0, m], m, 0, mine)
        relays[m].wait()
        unpack(edge.at[1, m], m, 0, theirs)
        add_edge(m)
        for j in range(2):
            for copy in parts(2 * m + j):
                copy.start()
        if m + 1 < members:
            edges[m + 1].wait()
            relays[m + 1].start()

    main = ffn // WIDE * WIDE
    extra = ffn - main
    at = 3 * fields + 3
    mix_top, mix_low = halves(w_mix[...])
    stacked = jnp.concatenate([mix_top, mix_low], axis=0).astype(jnp.bfloat16)
    load_in.wait()

    def product(cols):
        in_top, in_low = halves(w_in[:, cols])
        big = jnp.dot(stacked, in_top.astype(jnp.bfloat16), preferred_element_type=jnp.float32)
        small = jnp.dot(
            mix_top.astype(jnp.bfloat16), in_low.astype(jnp.bfloat16), preferred_element_type=jnp.float32
        )
        whole = big[:fields] + (big[fields:] + small)
        top, low = halves(whole)
        bias, leave = halves(b_in[cols][None, :])
        bias_low, leave = halves(leave)
        width = whole.shape[1]
        return jnp.concatenate(
            [top, low, top, bias, bias_low, leave, jnp.zeros((WIDE - at, width), jnp.float32)], axis=0
        )

    for c in range(main // WIDE):
        cols = slice(c * WIDE, (c + 1) * WIDE)
        first[:, cols] = product(cols).astype(jnp.bfloat16)
    tail = product(slice(main, ffn))
    rest[...] = jnp.concatenate(
        [jnp.zeros((WIDE, at), jnp.float32)]
        + [tail] * 3
        + [jnp.zeros((WIDE, WIDE - at - 3 * extra), jnp.float32)],
        axis=1,
    ).astype(jnp.bfloat16)
    load_out.wait()
    for c in range(main // WIDE):
        top, low = halves(w_out[:, c * WIDE : (c + 1) * WIDE].T)
        base = 3 * c * WIDE
        second[base : base + WIDE, :] = top.astype(jnp.bfloat16)
        second[base + WIDE : base + 2 * WIDE, :] = low.astype(jnp.bfloat16)
        second[base + 2 * WIDE : base + 3 * WIDE, :] = top.astype(jnp.bfloat16)
    top, low = halves(w_out[:, main:].T)
    second[3 * main :, :] = jnp.concatenate(
        [mix_top, mix_low, mix_top, jnp.zeros((3, embed), jnp.float32), top, low, top]
        + [jnp.zeros((WIDE - at - 3 * extra, embed), jnp.float32)],
        axis=0,
    ).astype(jnp.bfloat16)

    count = lon_dev // 2
    room = rows_f32.shape[1]
    for side in range(WIDE // LANES):
        rows_f32[side, count * GROUP :, :] = jnp.zeros((room - count * GROUP, LANES), jnp.float32)

    def finish_part(k):
        for copy in parts(k):
            copy.wait()
        v = [own[k, i] + incoming[0, k, i] + incoming[1, k, i] for i in range(GROUP - 1)]
        lane = lax.broadcasted_iota(jnp.int32, v[0].shape, 1)
        fields_of = [v[0]]
        for q in range(1, GROUP):
            both = v[q - 1] if q == GROUP - 1 else jnp.where(lane >= turns[q], v[q - 1], v[q])
            fields_of.append(pltpu.roll(both, LANES - turns[q], 1))
        for q in range(GROUP):
            top, low = halves(fields_of[q])
            flat = jnp.concatenate(
                [top, top, low, jnp.ones((3, LANES), jnp.float32)]
                + [jnp.zeros((WIDE - at, LANES), jnp.float32)],
                axis=0,
            )
            turned = flat.T[:count]
            for side in range(WIDE // LANES):
                rows_f32[side, pl.ds(q, count, stride=GROUP), :] = turned[
                    :, side * LANES : (side + 1) * LANES
                ]
        return jnp.concatenate([rows_f32[side] for side in range(WIDE // LANES)], axis=1).astype(
            jnp.bfloat16
        )

    def store_of(k):
        return pltpu.make_async_copy(result, early_out.at[k], result_sem)

    def piece(k, carry):
        left[...] = finish_part(k)
        total = mlp_rows(fields, extra, left[...], first, rest, second, held)

        @pl.when(k > 0)
        def _():
            store_of(k - 1).wait()

        result[...] = total[: count * GROUP].reshape(count, GROUP, embed)
        store_of(k).start()
        return carry

    lax.fori_loop(0, pieces, piece, 0)
    store_of(pieces - 1).wait()


def deliver(made, out, passing, in_sem, out_sem):
    pieces, count = made.shape[:2]
    inward = [pltpu.make_async_copy(made.at[k], passing.at[k], in_sem.at[k]) for k in range(pieces)]
    outward = [
        pltpu.make_async_copy(
            passing.at[k], out.at[k // 2, pl.ds(k % 2 * count, count)], out_sem.at[k]
        )
        for k in range(pieces)
    ]
    for copy in inward:
        copy.start()
    for come, go in zip(inward, outward):
        come.wait()
        go.start()
    for copy in outward:
        copy.wait()


def per_device_fast(bands, columns, state, kernels, kernel_index, w_mix, w_in, b_in, w_out):
    members, lat_dev, fields, lon_dev = state.shape
    lat_half = lat_dev // 2
    pieces = 2 * members
    count = lon_dev // 2
    embed, ffn = w_in.shape
    main = ffn // WIDE * WIDE
    depth = 3 * main + WIDE
    room = room_of(lon_dev)
    vmem = pl.BlockSpec(memory_space=pltpu.VMEM)
    hbm = pl.BlockSpec(memory_space=pl.ANY)
    f32 = jnp.float32
    half = jnp.bfloat16
    dma = pltpu.SemaphoreType.DMA
    packed = (pieces, GROUP - 1, fields, LANES)
    made = pl.pallas_call(
        functools.partial(exchange, bands, columns),
        out_shape=jax.ShapeDtypeStruct((pieces, count, GROUP, embed), f32),
        in_specs=[pl.BlockSpec(memory_space=pltpu.SMEM)] + [vmem] * 3 + [hbm] * 3,
        out_specs=hbm,
        scratch_shapes=[
            pltpu.VMEM(state.shape, f32),
            pltpu.VMEM(w_in.shape, f32),
            pltpu.VMEM(w_out.shape[::-1], f32),
            pltpu.VMEM((WIDE, main), half),
            pltpu.VMEM((WIDE, WIDE), half),
            pltpu.VMEM((depth, embed), half),
            pltpu.VMEM((room, WIDE), half),
            pltpu.VMEM((WIDE // LANES, room, LANES), f32),
            pltpu.VMEM((room, depth), half),
            pltpu.VMEM((count, GROUP, embed), f32),
            pltpu.VMEM(state.shape, f32),
            pltpu.VMEM((2, members, fields, lon_dev), f32),
            pltpu.VMEM((members, lat_dev + 1, 4, fields, LANES), f32),
            pltpu.VMEM((lat_half * 3, 2 * TAPS - 3, fields, LANES), f32),
            pltpu.VMEM(packed, f32),
            pltpu.VMEM((2,) + packed, f32),
            pltpu.VMEM((2,) + packed, f32),
            dma((members + 2,)),
            dma(()),
            dma((members,)),
            dma((members,)),
            dma((members,)),
            dma((members,)),
            dma((members,)),
            dma((members,)),
            dma((2, pieces)),
            dma((2, pieces)),
        ],
        compiler_params=pltpu.CompilerParams(
            collective_id=0, has_side_effects=True, vmem_limit_bytes=60 * 2**20
        ),
        name="exchange",
    )(
        kernel_index,
        jnp.transpose(kernels, (0, 2, 1, 3)),
        w_mix,
        b_in,
        state,
        w_in,
        w_out.T,
    )
    out = pl.pallas_call(
        deliver,
        out_shape=jax.ShapeDtypeStruct((members, lon_dev, lat_half, embed), f32),
        in_specs=[hbm],
        out_specs=hbm,
        scratch_shapes=[
            pltpu.VMEM((pieces, count, GROUP, embed), f32),
            dma((pieces,)),
            dma((pieces,)),
        ],
        compiler_params=pltpu.CompilerParams(vmem_limit_bytes=60 * 2**20),
        name="deliver",
    )(made)
    return jnp.transpose(out, (0, 2, 1, 3))


def fits(mesh, state, w_in):
    bands, columns = mesh.shape["polar"], mesh.shape["azimuth"]
    members, lat, fields, lon = state.shape
    main = w_in.shape[1] // WIDE * WIDE
    return (
        bands >= 2
        and columns % 2 == 0
        and columns >= 6
        and lon == 2 * SPACING * columns
        and lat == 2 * GROUP * bands
        and fields % SUB == 0
        and main > 0
        and 3 * fields + 3 + 3 * (w_in.shape[1] - main) <= WIDE
    )


def solution(mesh):
    placed = (P(None, "polar", None, "azimuth"), P(), P(), P(), P(), P(), P())

    def run(state, kernels, kernel_index, w_mix, w_in, b_in, w_out):
        body = per_device
        if fits(mesh, state, w_in):
            body = functools.partial(per_device_fast, mesh.shape["polar"], mesh.shape["azimuth"])
        return jax.shard_map(
            body,
            mesh=mesh,
            in_specs=placed,
            out_specs=P(None, "polar", "azimuth", None),
            check_vma=False,
        )(state, kernels, kernel_index, w_mix, w_in, b_in, w_out)

    return run
```

```python
import functools
import math

import jax
import jax.numpy as jnp
from jax import lax
from jax.experimental import pallas as pl
from jax.experimental.pallas import tpu as pltpu
from jax.sharding import PartitionSpec as P

TAPS = 9
SPACING = 90


def shifted(array, axis, by):
    peers = lax.axis_size(axis)
    pairs = [(i, i + by) for i in range(peers) if 0 <= i + by < peers]
    return lax.ppermute(array, axis, pairs)


def row_taps(kernels, kernel_index, out_lat, tap_pos, channel, valid):
    fields = kernels.shape[3]
    total_out = kernel_index.shape[0]
    pick = (out_lat[:, None] == jnp.arange(total_out, dtype=jnp.int32)[None, :]).astype(jnp.int32)
    kernel_of = jnp.sum(pick * kernel_index[None, :], axis=1)
    one_kernel = (
        kernel_of[:, None] == jnp.arange(kernels.shape[0], dtype=jnp.int32)[None, :]
    ).astype(jnp.float32)
    one_tap = (tap_pos[:, None] == jnp.arange(3, dtype=jnp.int32)[None, :]).astype(jnp.float32)
    one_field = (channel[:, None] == jnp.arange(fields, dtype=jnp.int32)[None, :]).astype(
        jnp.float32
    )
    chosen = jnp.einsum(
        "rk,ra,rc,katc->rt",
        one_kernel,
        one_tap,
        one_field,
        kernels,
        precision=lax.Precision.HIGHEST,
        preferred_element_type=jnp.float32,
    )
    return chosen * valid[:, None]


def correlate(cycle, weights):
    half = TAPS // 2
    total = jnp.zeros(cycle.shape, jnp.float32)
    for tap in range(TAPS):
        total = total + weights[:, tap : tap + 1] * jnp.roll(cycle, -(tap - half) * SPACING, axis=1)
    return total


def finish(summed, w_mix, w_in, b_in, w_out):
    lat_half, fields, lon_dev = summed.shape
    mixed = jnp.einsum(
        "ocl,ce->ole",
        summed,
        w_mix,
        precision=lax.Precision.HIGHEST,
        preferred_element_type=jnp.float32,
    ).reshape(lat_half * lon_dev, -1)
    pre = (
        jnp.dot(mixed, w_in, precision=lax.Precision.HIGHEST, preferred_element_type=jnp.float32)
        + b_in
    )
    hidden = jax.nn.gelu(pre, approximate=False)
    out = mixed + jnp.dot(
        hidden, w_out, precision=lax.Precision.HIGHEST, preferred_element_type=jnp.float32
    )
    return out.reshape(lat_half, lon_dev, -1)


def per_device(state, kernels, kernel_index, w_mix, w_in, b_in, w_out):
    members, lat_dev, fields, lon_dev = state.shape
    lat_half = lat_dev // 2
    azim = lax.axis_index("azimuth")
    band = lax.axis_index("polar")
    total_out = kernel_index.shape[0]
    results = []
    for member in range(members):
        block = state[member]
        flat = block.reshape(lat_dev * fields, lon_dev)
        cycle = lax.all_to_all(flat, "azimuth", split_axis=0, concat_axis=1, tiled=True)
        rows_here = cycle.shape[0]
        index = azim * rows_here + jnp.arange(rows_here, dtype=jnp.int32)
        glob = band * lat_dev + index // fields
        channel = index % fields
        parity = glob % 2
        first_w = row_taps(
            kernels,
            kernel_index,
            glob // 2,
            1 + parity,
            channel,
            jnp.ones((rows_here,), jnp.float32),
        )
        second_out = (glob + 1) // 2
        second_ok = ((parity == 1) & (second_out < total_out)).astype(jnp.float32)
        second_w = row_taps(
            kernels, kernel_index, second_out, jnp.zeros_like(glob), channel, second_ok
        )
        planes = jnp.stack([correlate(cycle, first_w), correlate(cycle, second_w)])
        back = lax.all_to_all(planes, "azimuth", split_axis=2, concat_axis=1, tiled=True)
        back = back.reshape(2, lat_half, 2, fields, lon_dev)
        near = back[0, :, 0] + back[0, :, 1]
        upper = back[1, :, 1]
        edge = shifted(upper[-1], "polar", 1)
        summed = near + jnp.concatenate([edge[None], upper[:-1]], axis=0)
        results.append(finish(summed, w_mix, w_in, b_in, w_out))
    return jnp.stack(results)


LANES = 128
SUB = 8
GROUP = 4
WIDE = 256
MESH = pl.DeviceIdType.MESH


def halves(x):
    top = x.astype(jnp.bfloat16).astype(jnp.float32)
    return top, x - top


def room_of(lon_dev):
    return -(-(lon_dev // 2 * GROUP) // 16) * 16


ERFC = (0.254829592, -0.284496736, 1.421413741, -1.453152027, 1.061405429)
ERFC_P = 0.3275911


def gelu(x):
    size = jnp.abs(x)
    base = size * (ERFC_P * 0.5**0.5) + 1.0
    guess = pl.reciprocal(base, approx=True)
    t = guess * (2.0 - base * guess)
    poly = ERFC[4] * 0.5
    for coefficient in ERFC[3::-1]:
        poly = poly * t + coefficient * 0.5
    upper = poly * t * jnp.exp2(x * x * (-0.5 / math.log(2.0)))
    return jnp.maximum(x, 0.0) - size * upper


def mlp_rows(fields, extra, left16, first, rest, second, held):
    chunks = first.shape[1] // WIDE
    at = 3 * fields + 3
    low_at = at + 2 * extra

    def act(weights):
        return gelu(jnp.dot(left16, weights, preferred_element_type=jnp.float32))

    total = None
    done = 0
    for c in range(chunks):
        hidden = act(first[:, c * WIDE : (c + 1) * WIDE])
        top = hidden.astype(jnp.bfloat16)
        low = (hidden - top.astype(jnp.float32)).astype(jnp.bfloat16)
        base = 3 * c * WIDE
        held[:, base : base + WIDE] = top
        held[:, base + WIDE : base + 2 * WIDE] = top
        held[:, base + 2 * WIDE : base + 3 * WIDE] = low
        if c == chunks - 1:
            top, low = halves(act(rest[...]))
            lane = lax.broadcasted_iota(jnp.int32, top.shape, 1)
            mixed = jnp.where(
                lane < at,
                left16.astype(jnp.float32),
                jnp.where(lane < low_at, top, jnp.where(lane < low_at + extra, low, 0.0)),
            )
            held[:, 3 * chunks * WIDE :] = mixed.astype(jnp.bfloat16)
        if c % 2 == 1 or c == chunks - 1:
            upto = base + 3 * WIDE if c < chunks - 1 else held.shape[1]
            term = jnp.dot(held[:, done:upto], second[done:upto, :], preferred_element_type=jnp.float32)
            total = term if total is None else total + term
            done = upto
    return total


def exchange(
    bands,
    columns,
    idx_ref,
    kern,
    w_mix,
    b_in,
    st_hbm,
    w_in_hbm,
    w_out_hbm,
    early_out,
    st,
    w_in,
    w_out,
    first,
    rest,
    second,
    left,
    rows_f32,
    held,
    result,
    peer,
    edge,
    blocks,
    taps,
    own,
    outgoing,
    incoming,
    load_sem,
    result_sem,
    peer_send,
    peer_recv,
    edge_send,
    edge_recv,
    relay_send,
    relay_recv,
    part_send,
    part_recv,
):
    members, lat_dev, fields, lon_dev = st.shape
    lat_half = lat_dev // 2
    tiles = fields // SUB
    embed, ffn = w_in.shape
    pieces = 2 * members
    az = lax.axis_index("azimuth")
    band = lax.axis_index("polar")
    core = lax.rem(az, 2)
    chip = az // 2
    chips = columns // 2
    mate = chip * 2 + 1 - core
    near = lax.rem(chip + chips - 1 + 2 * core, chips) * 2 + core
    far = lax.rem(chip + chips + 1 - 2 * core, chips) * 2 + core
    next_band = lax.rem(band + 1, bands)
    last_band = lax.rem(band + bands - 1, bands)

    loads = [pltpu.make_async_copy(st_hbm.at[m], st.at[m], load_sem.at[m]) for m in range(members)]
    load_in = pltpu.make_async_copy(w_in_hbm, w_in, load_sem.at[members])
    load_out = pltpu.make_async_copy(w_out_hbm, w_out, load_sem.at[members + 1])
    for copy in loads:
        copy.start()

    barrier = pltpu.get_barrier_semaphore()
    for who in ((band, mate), (band, near), (band, far), (last_band, az)):
        pl.semaphore_signal(barrier, inc=1, device_id=who, device_id_type=MESH)
    pl.semaphore_wait(barrier, 4)

    def remote(src, dst, send, recv, who):
        return pltpu.make_async_remote_copy(
            src_ref=src, dst_ref=dst, send_sem=send, recv_sem=recv, device_id=who, device_id_type=MESH
        )

    peers = []
    edges = []
    relays = []
    for m in range(members):
        peers.append(remote(st_hbm.at[m], peer.at[m], peer_send.at[m], peer_recv.at[m], (band, mate)))
        edges.append(
            remote(
                st_hbm.at[m, lat_dev - 1], edge.at[0, m], edge_send.at[m], edge_recv.at[m], (next_band, az)
            )
        )
        relays.append(
            remote(edge.at[0, m], edge.at[1, m], relay_send.at[m], relay_recv.at[m], (band, mate))
        )
    for m in range(members):
        edges[m].start()
        peers[m].start()
    load_in.start()
    load_out.start()

    half = TAPS // 2
    pad = half - 1
    for o in range(lat_half):
        k = idx_ref[band * lat_half + o]
        for a in range(3):
            columns_of = kern[k, :, a, :].T
            if o == 0 and a == 0:
                columns_of = columns_of * jnp.where(band > 0, 1.0, 0.0)
            for t in range(TAPS):
                taps[o * 3 + a, t + pad] = jnp.broadcast_to(columns_of[:, t : t + 1], (fields, LANES))
            for t in range(pad):
                taps[o * 3 + a, t] = jnp.zeros((fields, LANES), jnp.float32)
                taps[o * 3 + a, t + pad + TAPS] = jnp.zeros((fields, LANES), jnp.float32)

    spare = lon_dev - LANES

    def unpack(src, m, lat, to):
        x = src[:, :LANES]
        y = src[:, LANES:]
        y = jnp.concatenate([y, jnp.zeros((fields, LANES - spare), jnp.float32)], axis=1)
        lane = lax.broadcasted_iota(jnp.int32, x.shape, 1)
        blocks[m, lat, to] = x
        blocks[m, lat, to + 1] = pltpu.roll(jnp.where(lane < SPACING, y, x), LANES - SPACING, 1)

    turns = [q * SPACING % LANES for q in range(GROUP)]

    def pack(value, ref, at, rows):
        lane = lax.broadcasted_iota(jnp.int32, (SUB, LANES), 1)
        turned = [value[0]] + [pltpu.roll(value[q], turns[q], 1) for q in range(1, GROUP)]
        ref[at + (0, rows, slice(None))] = jnp.where(lane < turns[1], turned[0], turned[1])
        ref[at + (1, rows, slice(None))] = jnp.where(lane < turns[2], turned[1], turned[2])
        ref[at + (2, rows, slice(None))] = jnp.where(lane < turns[3], turned[2], turned[3])

    mine = 2 * core
    theirs = 2 - 2 * core
    plans = {
        "near": (2, mine, pad + 2 * half * (1 - core), lambda k: outgoing.at[0, k]),
        "far": (4, 0, pad + 2 * (half - 1) * core, lambda k: outgoing.at[1, k]),
        "own": (4, 0, pad + half - 2 * core, lambda k: own.at[k]),
    }

    def terms(x, tap, base, rows):
        w = {d: taps[tap, base + d, rows, :] for d in range(-1, len(x))}
        sums = []
        for j in range(2):
            term = w[-j] * x[0]
            for b in range(1, len(x)):
                term = term + w[b - j] * x[b]
            sums.append(term)
        return sums

    def correlate_part(m, plan, with_edge):
        width, start, base, ref_of = plans[plan]

        def body(r, carry):
            rows = pl.ds(pl.multiple_of(r * SUB, SUB), SUB)
            total = [[None] * lat_half for _ in range(2)]
            for o in range(lat_half):
                for a in range(1 if o == 0 and not with_edge else 0, 3):
                    x = [blocks[m, 2 * o + a, start + b, rows, :] for b in range(width)]
                    for j, term in enumerate(terms(x, o * 3 + a, base, rows)):
                        old = total[j][o]
                        total[j][o] = term if old is None else old + term
            for j in range(2):
                pack(total[j], ref_of(2 * m + j), (), rows)
            return carry

        lax.fori_loop(0, tiles, body, 0)

    def add_edge(m, plan):
        width, start, base, ref_of = plans[plan]

        def body(r, carry):
            rows = pl.ds(pl.multiple_of(r * SUB, SUB), SUB)
            lane = lax.broadcasted_iota(jnp.int32, (SUB, LANES), 1)
            x = [blocks[m, 0, start + b, rows, :] for b in range(width)]
            for j, term in enumerate(terms(x, 0, base, rows)):
                ref = ref_of(2 * m + j)
                ref[0, rows, :] = ref[0, rows, :] + jnp.where(lane < SPACING, term, 0.0)
            return carry

        lax.fori_loop(0, tiles, body, 0)

    def part(way, k):
        return remote(
            outgoing.at[way, k],
            incoming.at[way, k],
            part_send.at[way, k],
            part_recv.at[way, k],
            (band, (near, far)[way]),
        )

    for m in range(members):
        loads[m].wait()
        for lat in range(lat_dev):
            unpack(st.at[m, lat], m, lat + 1, mine)
        correlate_part(m, "near", False)
        edges[m].wait()
        relays[m].start()
        unpack(edge.at[0, m], m, 0, mine)
        add_edge(m, "near")
        for j in range(2):
            part(0, 2 * m + j).start()
        peers[m].wait()
        for lat in range(lat_dev):
            unpack(peer.at[m, lat], m, lat + 1, theirs)
        correlate_part(m, "far", False)
        relays[m].wait()
        unpack(edge.at[1, m], m, 0, theirs)
        add_edge(m, "far")
        for j in range(2):
            part(1, 2 * m + j).start()
    for m in range(members):
        correlate_part(m, "own", True)

    main = ffn // WIDE * WIDE
    extra = ffn - main
    at = 3 * fields + 3
    mix_top, mix_low = halves(w_mix[...])
    stacked = jnp.concatenate([mix_top, mix_low], axis=0).astype(jnp.bfloat16)
    load_in.wait()

    def product(cols):
        in_top, in_low = halves(w_in[:, cols])
        big = jnp.dot(stacked, in_top.astype(jnp.bfloat16), preferred_element_type=jnp.float32)
        small = jnp.dot(
            mix_top.astype(jnp.bfloat16), in_low.astype(jnp.bfloat16), preferred_element_type=jnp.float32
        )
        whole = big[:fields] + (big[fields:] + small)
        top, low = halves(whole)
        bias, leave = halves(b_in[cols][None, :])
        bias_low, leave = halves(leave)
        width = whole.shape[1]
        return jnp.concatenate(
            [top, low, top, bias, bias_low, leave, jnp.zeros((WIDE - at, width), jnp.float32)], axis=0
        )

    for c in range(main // WIDE):
        cols = slice(c * WIDE, (c + 1) * WIDE)
        first[:, cols] = product(cols).astype(jnp.bfloat16)
    tail = product(slice(main, ffn))
    rest[...] = jnp.concatenate(
        [jnp.zeros((WIDE, at), jnp.float32)]
        + [tail] * 3
        + [jnp.zeros((WIDE, WIDE - at - 3 * extra), jnp.float32)],
        axis=1,
    ).astype(jnp.bfloat16)
    load_out.wait()
    for c in range(main // WIDE):
        top, low = halves(w_out[:, c * WIDE : (c + 1) * WIDE].T)
        base = 3 * c * WIDE
        second[base : base + WIDE, :] = top.astype(jnp.bfloat16)
        second[base + WIDE : base + 2 * WIDE, :] = low.astype(jnp.bfloat16)
        second[base + 2 * WIDE : base + 3 * WIDE, :] = top.astype(jnp.bfloat16)
    top, low = halves(w_out[:, main:].T)
    second[3 * main :, :] = jnp.concatenate(
        [mix_top, mix_low, mix_top, jnp.zeros((3, embed), jnp.float32), top, low, top]
        + [jnp.zeros((WIDE - at - 3 * extra, embed), jnp.float32)],
        axis=0,
    ).astype(jnp.bfloat16)

    count = lon_dev // 2
    room = rows_f32.shape[1]
    for side in range(WIDE // LANES):
        rows_f32[side, count * GROUP :, :] = jnp.zeros((room - count * GROUP, LANES), jnp.float32)

    def finish_part(k):
        for way in range(2):
            part(way, k).wait()
        v = [own[k, i] + incoming[0, k, i] + incoming[1, k, i] for i in range(GROUP - 1)]
        lane = lax.broadcasted_iota(jnp.int32, v[0].shape, 1)
        fields_of = [v[0]]
        for q in range(1, GROUP):
            both = v[q - 1] if q == GROUP - 1 else jnp.where(lane >= turns[q], v[q - 1], v[q])
            fields_of.append(pltpu.roll(both, LANES - turns[q], 1))
        for q in range(GROUP):
            top, low = halves(fields_of[q])
            flat = jnp.concatenate(
                [top, top, low, jnp.ones((3, LANES), jnp.float32)]
                + [jnp.zeros((WIDE - at, LANES), jnp.float32)],
                axis=0,
            )
            turned = flat.T[:count]
            for side in range(WIDE // LANES):
                rows_f32[side, pl.ds(q, count, stride=GROUP), :] = turned[
                    :, side * LANES : (side + 1) * LANES
                ]
        return jnp.concatenate([rows_f32[side] for side in range(WIDE // LANES)], axis=1).astype(
            jnp.bfloat16
        )

    def store_of(k):
        return pltpu.make_async_copy(result, early_out.at[k], result_sem)

    def piece(k, carry):
        left[...] = finish_part(k)
        total = mlp_rows(fields, extra, left[...], first, rest, second, held)

        @pl.when(k > 0)
        def _():
            store_of(k - 1).wait()

        result[...] = total[: count * GROUP].reshape(count, GROUP, embed)
        store_of(k).start()
        return carry

    lax.fori_loop(0, pieces, piece, 0)
    store_of(pieces - 1).wait()


def deliver(cuts, made, out, passing, in_sem, out_sem):
    pieces, count = made.shape[:2]
    step = count // cuts
    inward = []
    outward = []
    for k in range(pieces):
        for c in range(cuts):
            rows = pl.ds(c * step, step)
            i = k * cuts + c
            inward.append(pltpu.make_async_copy(made.at[k, rows], passing.at[k, rows], in_sem.at[i]))
            outward.append(
                pltpu.make_async_copy(
                    passing.at[k, rows],
                    out.at[k // 2, pl.ds(k % 2 * count + c * step, step)],
                    out_sem.at[i],
                )
            )
    for copy in inward:
        copy.start()
    for come, go in zip(inward, outward):
        come.wait()
        go.start()
    for copy in outward:
        copy.wait()


def per_device_fast(bands, columns, state, kernels, kernel_index, w_mix, w_in, b_in, w_out):
    members, lat_dev, fields, lon_dev = state.shape
    lat_half = lat_dev // 2
    pieces = 2 * members
    count = lon_dev // 2
    embed, ffn = w_in.shape
    main = ffn // WIDE * WIDE
    depth = 3 * main + WIDE
    room = room_of(lon_dev)
    vmem = pl.BlockSpec(memory_space=pltpu.VMEM)
    hbm = pl.BlockSpec(memory_space=pl.ANY)
    f32 = jnp.float32
    half = jnp.bfloat16
    dma = pltpu.SemaphoreType.DMA
    packed = (pieces, GROUP - 1, fields, LANES)
    made = pl.pallas_call(
        functools.partial(exchange, bands, columns),
        out_shape=jax.ShapeDtypeStruct((pieces, count, GROUP, embed), f32),
        in_specs=[pl.BlockSpec(memory_space=pltpu.SMEM)] + [vmem] * 3 + [hbm] * 3,
        out_specs=hbm,
        scratch_shapes=[
            pltpu.VMEM(state.shape, f32),
            pltpu.VMEM(w_in.shape, f32),
            pltpu.VMEM(w_out.shape[::-1], f32),
            pltpu.VMEM((WIDE, main), half),
            pltpu.VMEM((WIDE, WIDE), half),
            pltpu.VMEM((depth, embed), half),
            pltpu.VMEM((room, WIDE), half),
            pltpu.VMEM((WIDE // LANES, room, LANES), f32),
            pltpu.VMEM((room, depth), half),
            pltpu.VMEM((count, GROUP, embed), f32),
            pltpu.VMEM(state.shape, f32),
            pltpu.VMEM((2, members, fields, lon_dev), f32),
            pltpu.VMEM((members, lat_dev + 1, 4, fields, LANES), f32),
            pltpu.VMEM((lat_half * 3, 2 * TAPS - 3, fields, LANES), f32),
            pltpu.VMEM(packed, f32),
            pltpu.VMEM((2,) + packed, f32),
            pltpu.VMEM((2,) + packed, f32),
            dma((members + 2,)),
            dma(()),
            dma((members,)),
            dma((members,)),
            dma((members,)),
            dma((members,)),
            dma((members,)),
            dma((members,)),
            dma((2, pieces)),
            dma((2, pieces)),
        ],
        compiler_params=pltpu.CompilerParams(
            collective_id=0, has_side_effects=True, vmem_limit_bytes=60 * 2**20
        ),
        name="exchange",
    )(
        kernel_index,
        jnp.transpose(kernels, (0, 2, 1, 3)),
        w_mix,
        b_in,
        state,
        w_in,
        w_out.T,
    )
    cuts = 3 if count % 3 == 0 else 1
    out = pl.pallas_call(
        functools.partial(deliver, cuts),
        out_shape=jax.ShapeDtypeStruct((members, lon_dev, lat_half, embed), f32),
        in_specs=[hbm],
        out_specs=hbm,
        scratch_shapes=[
            pltpu.VMEM((pieces, count, GROUP, embed), f32),
            dma((pieces * cuts,)),
            dma((pieces * cuts,)),
        ],
        compiler_params=pltpu.CompilerParams(vmem_limit_bytes=60 * 2**20),
        name="deliver",
    )(made)
    return jnp.transpose(out, (0, 2, 1, 3))


def fits(mesh, state, w_in):
    bands, columns = mesh.shape["polar"], mesh.shape["azimuth"]
    members, lat, fields, lon = state.shape
    main = w_in.shape[1] // WIDE * WIDE
    return (
        bands >= 2
        and columns % 2 == 0
        and columns >= 6
        and lon == 2 * SPACING * columns
        and lat == 2 * GROUP * bands
        and fields % SUB == 0
        and main > 0
        and 3 * fields + 3 + 3 * (w_in.shape[1] - main) <= WIDE
    )


def solution(mesh):
    placed = (P(None, "polar", None, "azimuth"), P(), P(), P(), P(), P(), P())

    def run(state, kernels, kernel_index, w_mix, w_in, b_in, w_out):
        body = per_device
        if fits(mesh, state, w_in):
            body = functools.partial(per_device_fast, mesh.shape["polar"], mesh.shape["azimuth"])
        return jax.shard_map(
            body,
            mesh=mesh,
            in_specs=placed,
            out_specs=P(None, "polar", "azimuth", None),
            check_vma=False,
        )(state, kernels, kernel_index, w_mix, w_in, b_in, w_out)

    return run
```

```python
import functools
import math

import jax
import jax.numpy as jnp
from jax import lax
from jax.experimental import pallas as pl
from jax.experimental.pallas import tpu as pltpu
from jax.sharding import PartitionSpec as P

TAPS = 9
SPACING = 90


def shifted(array, axis, by):
    peers = lax.axis_size(axis)
    pairs = [(i, i + by) for i in range(peers) if 0 <= i + by < peers]
    return lax.ppermute(array, axis, pairs)


def row_taps(kernels, kernel_index, out_lat, tap_pos, channel, valid):
    fields = kernels.shape[3]
    total_out = kernel_index.shape[0]
    pick = (out_lat[:, None] == jnp.arange(total_out, dtype=jnp.int32)[None, :]).astype(jnp.int32)
    kernel_of = jnp.sum(pick * kernel_index[None, :], axis=1)
    one_kernel = (
        kernel_of[:, None] == jnp.arange(kernels.shape[0], dtype=jnp.int32)[None, :]
    ).astype(jnp.float32)
    one_tap = (tap_pos[:, None] == jnp.arange(3, dtype=jnp.int32)[None, :]).astype(jnp.float32)
    one_field = (channel[:, None] == jnp.arange(fields, dtype=jnp.int32)[None, :]).astype(
        jnp.float32
    )
    chosen = jnp.einsum(
        "rk,ra,rc,katc->rt",
        one_kernel,
        one_tap,
        one_field,
        kernels,
        precision=lax.Precision.HIGHEST,
        preferred_element_type=jnp.float32,
    )
    return chosen * valid[:, None]


def correlate(cycle, weights):
    half = TAPS // 2
    total = jnp.zeros(cycle.shape, jnp.float32)
    for tap in range(TAPS):
        total = total + weights[:, tap : tap + 1] * jnp.roll(cycle, -(tap - half) * SPACING, axis=1)
    return total


def finish(summed, w_mix, w_in, b_in, w_out):
    lat_half, fields, lon_dev = summed.shape
    mixed = jnp.einsum(
        "ocl,ce->ole",
        summed,
        w_mix,
        precision=lax.Precision.HIGHEST,
        preferred_element_type=jnp.float32,
    ).reshape(lat_half * lon_dev, -1)
    pre = (
        jnp.dot(mixed, w_in, precision=lax.Precision.HIGHEST, preferred_element_type=jnp.float32)
        + b_in
    )
    hidden = jax.nn.gelu(pre, approximate=False)
    out = mixed + jnp.dot(
        hidden, w_out, precision=lax.Precision.HIGHEST, preferred_element_type=jnp.float32
    )
    return out.reshape(lat_half, lon_dev, -1)


def per_device(state, kernels, kernel_index, w_mix, w_in, b_in, w_out):
    members, lat_dev, fields, lon_dev = state.shape
    lat_half = lat_dev // 2
    azim = lax.axis_index("azimuth")
    band = lax.axis_index("polar")
    total_out = kernel_index.shape[0]
    results = []
    for member in range(members):
        block = state[member]
        flat = block.reshape(lat_dev * fields, lon_dev)
        cycle = lax.all_to_all(flat, "azimuth", split_axis=0, concat_axis=1, tiled=True)
        rows_here = cycle.shape[0]
        index = azim * rows_here + jnp.arange(rows_here, dtype=jnp.int32)
        glob = band * lat_dev + index // fields
        channel = index % fields
        parity = glob % 2
        first_w = row_taps(
            kernels,
            kernel_index,
            glob // 2,
            1 + parity,
            channel,
            jnp.ones((rows_here,), jnp.float32),
        )
        second_out = (glob + 1) // 2
        second_ok = ((parity == 1) & (second_out < total_out)).astype(jnp.float32)
        second_w = row_taps(
            kernels, kernel_index, second_out, jnp.zeros_like(glob), channel, second_ok
        )
        planes = jnp.stack([correlate(cycle, first_w), correlate(cycle, second_w)])
        back = lax.all_to_all(planes, "azimuth", split_axis=2, concat_axis=1, tiled=True)
        back = back.reshape(2, lat_half, 2, fields, lon_dev)
        near = back[0, :, 0] + back[0, :, 1]
        upper = back[1, :, 1]
        edge = shifted(upper[-1], "polar", 1)
        summed = near + jnp.concatenate([edge[None], upper[:-1]], axis=0)
        results.append(finish(summed, w_mix, w_in, b_in, w_out))
    return jnp.stack(results)


LANES = 128
SUB = 8
GROUP = 4
WIDE = 256
MESH = pl.DeviceIdType.MESH


def halves(x):
    top = x.astype(jnp.bfloat16).astype(jnp.float32)
    return top, x - top


def room_of(lon_dev):
    return -(-(lon_dev // 2 * GROUP) // 16) * 16


ERFC = (0.254829592, -0.284496736, 1.421413741, -1.453152027, 1.061405429)
ERFC_P = 0.3275911


def gelu(x):
    size = jnp.abs(x)
    base = size * (ERFC_P * 0.5**0.5) + 1.0
    guess = pl.reciprocal(base, approx=True)
    t = guess * (2.0 - base * guess)
    poly = ERFC[4] * 0.5
    for coefficient in ERFC[3::-1]:
        poly = poly * t + coefficient * 0.5
    upper = poly * t * jnp.exp2(x * x * (-0.5 / math.log(2.0)))
    return jnp.maximum(x, 0.0) - size * upper


def mlp_rows(fields, extra, left16, first, rest, second, held):
    chunks = first.shape[1] // WIDE
    at = 3 * fields + 3
    low_at = at + 2 * extra

    def act(weights):
        return gelu(jnp.dot(left16, weights, preferred_element_type=jnp.float32))

    total = None
    done = 0
    for c in range(chunks):
        hidden = act(first[:, c * WIDE : (c + 1) * WIDE])
        top = hidden.astype(jnp.bfloat16)
        low = (hidden - top.astype(jnp.float32)).astype(jnp.bfloat16)
        base = 3 * c * WIDE
        held[:, base : base + WIDE] = top
        held[:, base + WIDE : base + 2 * WIDE] = top
        held[:, base + 2 * WIDE : base + 3 * WIDE] = low
        if c == chunks - 1:
            top, low = halves(act(rest[...]))
            lane = lax.broadcasted_iota(jnp.int32, top.shape, 1)
            mixed = jnp.where(
                lane < at,
                left16.astype(jnp.float32),
                jnp.where(lane < low_at, top, jnp.where(lane < low_at + extra, low, 0.0)),
            )
            held[:, 3 * chunks * WIDE :] = mixed.astype(jnp.bfloat16)
        if c % 2 == 1 or c == chunks - 1:
            upto = base + 3 * WIDE if c < chunks - 1 else held.shape[1]
            term = jnp.dot(held[:, done:upto], second[done:upto, :], preferred_element_type=jnp.float32)
            total = term if total is None else total + term
            done = upto
    return total


def exchange(
    bands,
    columns,
    idx_ref,
    kern,
    w_mix,
    b_in,
    st_hbm,
    w_in_hbm,
    w_out_hbm,
    early_out,
    st,
    w_in,
    w_out,
    first,
    rest,
    second,
    left,
    rows_f32,
    held,
    result,
    peer,
    edge,
    blocks,
    taps,
    own,
    outgoing,
    incoming,
    load_sem,
    result_sem,
    peer_send,
    peer_recv,
    edge_send,
    edge_recv,
    relay_send,
    relay_recv,
    part_send,
    part_recv,
):
    members, lat_dev, fields, lon_dev = st.shape
    lat_half = lat_dev // 2
    tiles = fields // SUB
    embed, ffn = w_in.shape
    pieces = 2 * members
    az = lax.axis_index("azimuth")
    band = lax.axis_index("polar")
    core = lax.rem(az, 2)
    chip = az // 2
    chips = columns // 2
    mate = chip * 2 + 1 - core
    near = lax.rem(chip + chips - 1 + 2 * core, chips) * 2 + core
    far = lax.rem(chip + chips + 1 - 2 * core, chips) * 2 + core
    next_band = lax.rem(band + 1, bands)
    last_band = lax.rem(band + bands - 1, bands)

    loads = [pltpu.make_async_copy(st_hbm.at[m], st.at[m], load_sem.at[m]) for m in range(members)]
    load_in = pltpu.make_async_copy(w_in_hbm, w_in, load_sem.at[members])
    load_out = pltpu.make_async_copy(w_out_hbm, w_out, load_sem.at[members + 1])
    for copy in loads:
        copy.start()

    barrier = pltpu.get_barrier_semaphore()
    for who in ((band, mate), (band, near), (band, far), (last_band, az)):
        pl.semaphore_signal(barrier, inc=1, device_id=who, device_id_type=MESH)
    pl.semaphore_wait(barrier, 4)

    def remote(src, dst, send, recv, who):
        return pltpu.make_async_remote_copy(
            src_ref=src, dst_ref=dst, send_sem=send, recv_sem=recv, device_id=who, device_id_type=MESH
        )

    peers = []
    edges = []
    relays = []
    for m in range(members):
        peers.append(remote(st_hbm.at[m], peer.at[m], peer_send.at[m], peer_recv.at[m], (band, mate)))
        edges.append(
            remote(
                st_hbm.at[m, lat_dev - 1], edge.at[0, m], edge_send.at[m], edge_recv.at[m], (next_band, az)
            )
        )
        relays.append(
            remote(edge.at[0, m], edge.at[1, m], relay_send.at[m], relay_recv.at[m], (band, mate))
        )
    for m in range(members):
        edges[m].start()
        peers[m].start()
    load_in.start()
    load_out.start()

    half = TAPS // 2
    pad = half - 1
    for o in range(lat_half):
        k = idx_ref[band * lat_half + o]
        for a in range(3):
            columns_of = kern[k, :, a, :].T
            if o == 0 and a == 0:
                columns_of = columns_of * jnp.where(band > 0, 1.0, 0.0)
            for t in range(TAPS):
                taps[o * 3 + a, t + pad] = jnp.broadcast_to(columns_of[:, t : t + 1], (fields, LANES))
            for t in range(pad):
                taps[o * 3 + a, t] = jnp.zeros((fields, LANES), jnp.float32)
                taps[o * 3 + a, t + pad + TAPS] = jnp.zeros((fields, LANES), jnp.float32)

    spare = lon_dev - LANES

    def unpack(src, m, lat, to):
        x = src[:, :LANES]
        y = src[:, LANES:]
        y = jnp.concatenate([y, jnp.zeros((fields, LANES - spare), jnp.float32)], axis=1)
        lane = lax.broadcasted_iota(jnp.int32, x.shape, 1)
        blocks[m, lat, to] = x
        blocks[m, lat, to + 1] = pltpu.roll(jnp.where(lane < SPACING, y, x), LANES - SPACING, 1)

    turns = [q * SPACING % LANES for q in range(GROUP)]

    def pack(value, ref, at, rows):
        lane = lax.broadcasted_iota(jnp.int32, (SUB, LANES), 1)
        turned = [value[0]] + [pltpu.roll(value[q], turns[q], 1) for q in range(1, GROUP)]
        ref[at + (0, rows, slice(None))] = jnp.where(lane < turns[1], turned[0], turned[1])
        ref[at + (1, rows, slice(None))] = jnp.where(lane < turns[2], turned[1], turned[2])
        ref[at + (2, rows, slice(None))] = jnp.where(lane < turns[3], turned[2], turned[3])

    mine = 2 * core
    theirs = 2 - 2 * core
    plans = {
        "near": (2, mine, pad + 2 * half * (1 - core), lambda k: outgoing.at[0, k]),
        "far": (4, 0, pad + 2 * (half - 1) * core, lambda k: outgoing.at[1, k]),
        "own": (4, 0, pad + half - 2 * core, lambda k: own.at[k]),
    }

    def terms(x, tap, base, rows):
        w = {d: taps[tap, base + d, rows, :] for d in range(-1, len(x))}
        sums = []
        for j in range(2):
            term = w[-j] * x[0]
            for b in range(1, len(x)):
                term = term + w[b - j] * x[b]
            sums.append(term)
        return sums

    def correlate_part(m, plan, with_edge):
        width, start, base, ref_of = plans[plan]

        def body(r, carry):
            rows = pl.ds(pl.multiple_of(r * SUB, SUB), SUB)
            total = [[None] * lat_half for _ in range(2)]
            for o in range(lat_half):
                for a in range(1 if o == 0 and not with_edge else 0, 3):
                    x = [blocks[m, 2 * o + a, start + b, rows, :] for b in range(width)]
                    for j, term in enumerate(terms(x, o * 3 + a, base, rows)):
                        old = total[j][o]
                        total[j][o] = term if old is None else old + term
            for j in range(2):
                pack(total[j], ref_of(2 * m + j), (), rows)
            return carry

        lax.fori_loop(0, tiles, body, 0)

    def add_edge(m, plan):
        width, start, base, ref_of = plans[plan]

        def body(r, carry):
            rows = pl.ds(pl.multiple_of(r * SUB, SUB), SUB)
            lane = lax.broadcasted_iota(jnp.int32, (SUB, LANES), 1)
            x = [blocks[m, 0, start + b, rows, :] for b in range(width)]
            for j, term in enumerate(terms(x, 0, base, rows)):
                ref = ref_of(2 * m + j)
                ref[0, rows, :] = ref[0, rows, :] + jnp.where(lane < SPACING, term, 0.0)
            return carry

        lax.fori_loop(0, tiles, body, 0)

    def part(way, k):
        return remote(
            outgoing.at[way, k],
            incoming.at[way, k],
            part_send.at[way, k],
            part_recv.at[way, k],
            (band, (near, far)[way]),
        )

    for m in range(members):
        loads[m].wait()
        for lat in range(lat_dev):
            unpack(st.at[m, lat], m, lat + 1, mine)
        correlate_part(m, "near", False)
        edges[m].wait()
        relays[m].start()
        unpack(edge.at[0, m], m, 0, mine)
        add_edge(m, "near")
        if m == 0:
            for j in range(2):
                part(0, j).start()
        peers[m].wait()
        for lat in range(lat_dev):
            unpack(peer.at[m, lat], m, lat + 1, theirs)
        correlate_part(m, "far", False)
        relays[m].wait()
        unpack(edge.at[1, m], m, 0, theirs)
        add_edge(m, "far")
        if m == 0:
            for j in range(2):
                part(1, j).start()
    for m in range(members):
        correlate_part(m, "own", True)

    def follow(k):
        for way in range(2):
            part(way, k - 2).wait_send()
        for way in range(2):
            part(way, k).start()

    main = ffn // WIDE * WIDE
    extra = ffn - main
    at = 3 * fields + 3
    mix_top, mix_low = halves(w_mix[...])
    stacked = jnp.concatenate([mix_top, mix_low], axis=0).astype(jnp.bfloat16)
    load_in.wait()

    def product(cols):
        in_top, in_low = halves(w_in[:, cols])
        big = jnp.dot(stacked, in_top.astype(jnp.bfloat16), preferred_element_type=jnp.float32)
        small = jnp.dot(
            mix_top.astype(jnp.bfloat16), in_low.astype(jnp.bfloat16), preferred_element_type=jnp.float32
        )
        whole = big[:fields] + (big[fields:] + small)
        top, low = halves(whole)
        bias, leave = halves(b_in[cols][None, :])
        bias_low, leave = halves(leave)
        width = whole.shape[1]
        return jnp.concatenate(
            [top, low, top, bias, bias_low, leave, jnp.zeros((WIDE - at, width), jnp.float32)], axis=0
        )

    for c in range(main // WIDE):
        cols = slice(c * WIDE, (c + 1) * WIDE)
        first[:, cols] = product(cols).astype(jnp.bfloat16)
    tail = product(slice(main, ffn))
    rest[...] = jnp.concatenate(
        [jnp.zeros((WIDE, at), jnp.float32)]
        + [tail] * 3
        + [jnp.zeros((WIDE, WIDE - at - 3 * extra), jnp.float32)],
        axis=1,
    ).astype(jnp.bfloat16)
    follow(2)
    load_out.wait()
    for c in range(main // WIDE):
        top, low = halves(w_out[:, c * WIDE : (c + 1) * WIDE].T)
        base = 3 * c * WIDE
        second[base : base + WIDE, :] = top.astype(jnp.bfloat16)
        second[base + WIDE : base + 2 * WIDE, :] = low.astype(jnp.bfloat16)
        second[base + 2 * WIDE : base + 3 * WIDE, :] = top.astype(jnp.bfloat16)
    top, low = halves(w_out[:, main:].T)
    second[3 * main :, :] = jnp.concatenate(
        [mix_top, mix_low, mix_top, jnp.zeros((3, embed), jnp.float32), top, low, top]
        + [jnp.zeros((WIDE - at - 3 * extra, embed), jnp.float32)],
        axis=0,
    ).astype(jnp.bfloat16)

    for k in range(3, pieces):
        follow(k)
    count = lon_dev // 2
    room = rows_f32.shape[1]
    for side in range(WIDE // LANES):
        rows_f32[side, count * GROUP :, :] = jnp.zeros((room - count * GROUP, LANES), jnp.float32)

    def finish_part(k):
        for way in range(2):
            part(way, k).wait_recv()
        v = [own[k, i] + incoming[0, k, i] + incoming[1, k, i] for i in range(GROUP - 1)]
        lane = lax.broadcasted_iota(jnp.int32, v[0].shape, 1)
        fields_of = [v[0]]
        for q in range(1, GROUP):
            both = v[q - 1] if q == GROUP - 1 else jnp.where(lane >= turns[q], v[q - 1], v[q])
            fields_of.append(pltpu.roll(both, LANES - turns[q], 1))
        for q in range(GROUP):
            top, low = halves(fields_of[q])
            flat = jnp.concatenate(
                [top, top, low, jnp.ones((3, LANES), jnp.float32)]
                + [jnp.zeros((WIDE - at, LANES), jnp.float32)],
                axis=0,
            )
            turned = flat.T[:count]
            for side in range(WIDE // LANES):
                rows_f32[side, pl.ds(q, count, stride=GROUP), :] = turned[
                    :, side * LANES : (side + 1) * LANES
                ]
        return jnp.concatenate([rows_f32[side] for side in range(WIDE // LANES)], axis=1).astype(
            jnp.bfloat16
        )

    def store_of(k):
        return pltpu.make_async_copy(result, early_out.at[k], result_sem)

    def piece(k, carry):
        left[...] = finish_part(k)
        total = mlp_rows(fields, extra, left[...], first, rest, second, held)

        @pl.when(k > 0)
        def _():
            store_of(k - 1).wait()

        result[...] = total[: count * GROUP].reshape(count, GROUP, embed)
        store_of(k).start()
        return carry

    lax.fori_loop(0, pieces, piece, 0)
    for k in range(pieces - 2, pieces):
        for way in range(2):
            part(way, k).wait_send()
    store_of(pieces - 1).wait()


def deliver(cuts, made, out, passing, in_sem, out_sem):
    pieces, count = made.shape[:2]
    step = count // cuts
    inward = []
    outward = []
    for k in range(pieces):
        for c in range(cuts):
            rows = pl.ds(c * step, step)
            i = k * cuts + c
            inward.append(pltpu.make_async_copy(made.at[k, rows], passing.at[k, rows], in_sem.at[i]))
            outward.append(
                pltpu.make_async_copy(
                    passing.at[k, rows],
                    out.at[k // 2, pl.ds(k % 2 * count + c * step, step)],
                    out_sem.at[i],
                )
            )
    for copy in inward:
        copy.start()
    for come, go in zip(inward, outward):
        come.wait()
        go.start()
    for copy in outward:
        copy.wait()


def per_device_fast(bands, columns, state, kernels, kernel_index, w_mix, w_in, b_in, w_out):
    members, lat_dev, fields, lon_dev = state.shape
    lat_half = lat_dev // 2
    pieces = 2 * members
    count = lon_dev // 2
    embed, ffn = w_in.shape
    main = ffn // WIDE * WIDE
    depth = 3 * main + WIDE
    room = room_of(lon_dev)
    vmem = pl.BlockSpec(memory_space=pltpu.VMEM)
    hbm = pl.BlockSpec(memory_space=pl.ANY)
    f32 = jnp.float32
    half = jnp.bfloat16
    dma = pltpu.SemaphoreType.DMA
    packed = (pieces, GROUP - 1, fields, LANES)
    made = pl.pallas_call(
        functools.partial(exchange, bands, columns),
        out_shape=jax.ShapeDtypeStruct((pieces, count, GROUP, embed), f32),
        in_specs=[pl.BlockSpec(memory_space=pltpu.SMEM)] + [vmem] * 3 + [hbm] * 3,
        out_specs=hbm,
        scratch_shapes=[
            pltpu.VMEM(state.shape, f32),
            pltpu.VMEM(w_in.shape, f32),
            pltpu.VMEM(w_out.shape[::-1], f32),
            pltpu.VMEM((WIDE, main), half),
            pltpu.VMEM((WIDE, WIDE), half),
            pltpu.VMEM((depth, embed), half),
            pltpu.VMEM((room, WIDE), half),
            pltpu.VMEM((WIDE // LANES, room, LANES), f32),
            pltpu.VMEM((room, depth), half),
            pltpu.VMEM((count, GROUP, embed), f32),
            pltpu.VMEM(state.shape, f32),
            pltpu.VMEM((2, members, fields, lon_dev), f32),
            pltpu.VMEM((members, lat_dev + 1, 4, fields, LANES), f32),
            pltpu.VMEM((lat_half * 3, 2 * TAPS - 3, fields, LANES), f32),
            pltpu.VMEM(packed, f32),
            pltpu.VMEM((2,) + packed, f32),
            pltpu.VMEM((2,) + packed, f32),
            dma((members + 2,)),
            dma(()),
            dma((members,)),
            dma((members,)),
            dma((members,)),
            dma((members,)),
            dma((members,)),
            dma((members,)),
            dma((2, pieces)),
            dma((2, pieces)),
        ],
        compiler_params=pltpu.CompilerParams(
            collective_id=0, has_side_effects=True, vmem_limit_bytes=60 * 2**20
        ),
        name="exchange",
    )(
        kernel_index,
        jnp.transpose(kernels, (0, 2, 1, 3)),
        w_mix,
        b_in,
        state,
        w_in,
        w_out.T,
    )
    cuts = 1
    out = pl.pallas_call(
        functools.partial(deliver, cuts),
        out_shape=jax.ShapeDtypeStruct((members, lon_dev, lat_half, embed), f32),
        in_specs=[hbm],
        out_specs=hbm,
        scratch_shapes=[
            pltpu.VMEM((pieces, count, GROUP, embed), f32),
            dma((pieces * cuts,)),
            dma((pieces * cuts,)),
        ],
        compiler_params=pltpu.CompilerParams(vmem_limit_bytes=60 * 2**20),
        name="deliver",
    )(made)
    return jnp.transpose(out, (0, 2, 1, 3))


def fits(mesh, state, w_in):
    bands, columns = mesh.shape["polar"], mesh.shape["azimuth"]
    members, lat, fields, lon = state.shape
    main = w_in.shape[1] // WIDE * WIDE
    return (
        bands >= 2
        and columns % 2 == 0
        and columns >= 6
        and lon == 2 * SPACING * columns
        and lat == 2 * GROUP * bands
        and fields % SUB == 0
        and main > 0
        and 3 * fields + 3 + 3 * (w_in.shape[1] - main) <= WIDE
    )


def solution(mesh):
    placed = (P(None, "polar", None, "azimuth"), P(), P(), P(), P(), P(), P())

    def run(state, kernels, kernel_index, w_mix, w_in, b_in, w_out):
        body = per_device
        if fits(mesh, state, w_in):
            body = functools.partial(per_device_fast, mesh.shape["polar"], mesh.shape["azimuth"])
        return jax.shard_map(
            body,
            mesh=mesh,
            in_specs=placed,
            out_specs=P(None, "polar", "azimuth", None),
            check_vma=False,
        )(state, kernels, kernel_index, w_mix, w_in, b_in, w_out)

    return run
```

```python
import functools
import math

import jax
import jax.numpy as jnp
from jax import lax
from jax.experimental import pallas as pl
from jax.experimental.pallas import tpu as pltpu
from jax.sharding import PartitionSpec as P

TAPS = 9
SPACING = 90


def shifted(array, axis, by):
    peers = lax.axis_size(axis)
    pairs = [(i, i + by) for i in range(peers) if 0 <= i + by < peers]
    return lax.ppermute(array, axis, pairs)


def row_taps(kernels, kernel_index, out_lat, tap_pos, channel, valid):
    fields = kernels.shape[3]
    total_out = kernel_index.shape[0]
    pick = (out_lat[:, None] == jnp.arange(total_out, dtype=jnp.int32)[None, :]).astype(jnp.int32)
    kernel_of = jnp.sum(pick * kernel_index[None, :], axis=1)
    one_kernel = (
        kernel_of[:, None] == jnp.arange(kernels.shape[0], dtype=jnp.int32)[None, :]
    ).astype(jnp.float32)
    one_tap = (tap_pos[:, None] == jnp.arange(3, dtype=jnp.int32)[None, :]).astype(jnp.float32)
    one_field = (channel[:, None] == jnp.arange(fields, dtype=jnp.int32)[None, :]).astype(
        jnp.float32
    )
    chosen = jnp.einsum(
        "rk,ra,rc,katc->rt",
        one_kernel,
        one_tap,
        one_field,
        kernels,
        precision=lax.Precision.HIGHEST,
        preferred_element_type=jnp.float32,
    )
    return chosen * valid[:, None]


def correlate(cycle, weights):
    half = TAPS // 2
    total = jnp.zeros(cycle.shape, jnp.float32)
    for tap in range(TAPS):
        total = total + weights[:, tap : tap + 1] * jnp.roll(cycle, -(tap - half) * SPACING, axis=1)
    return total


def finish(summed, w_mix, w_in, b_in, w_out):
    lat_half, fields, lon_dev = summed.shape
    mixed = jnp.einsum(
        "ocl,ce->ole",
        summed,
        w_mix,
        precision=lax.Precision.HIGHEST,
        preferred_element_type=jnp.float32,
    ).reshape(lat_half * lon_dev, -1)
    pre = (
        jnp.dot(mixed, w_in, precision=lax.Precision.HIGHEST, preferred_element_type=jnp.float32)
        + b_in
    )
    hidden = jax.nn.gelu(pre, approximate=False)
    out = mixed + jnp.dot(
        hidden, w_out, precision=lax.Precision.HIGHEST, preferred_element_type=jnp.float32
    )
    return out.reshape(lat_half, lon_dev, -1)


def per_device(state, kernels, kernel_index, w_mix, w_in, b_in, w_out):
    members, lat_dev, fields, lon_dev = state.shape
    lat_half = lat_dev // 2
    azim = lax.axis_index("azimuth")
    band = lax.axis_index("polar")
    total_out = kernel_index.shape[0]
    results = []
    for member in range(members):
        block = state[member]
        flat = block.reshape(lat_dev * fields, lon_dev)
        cycle = lax.all_to_all(flat, "azimuth", split_axis=0, concat_axis=1, tiled=True)
        rows_here = cycle.shape[0]
        index = azim * rows_here + jnp.arange(rows_here, dtype=jnp.int32)
        glob = band * lat_dev + index // fields
        channel = index % fields
        parity = glob % 2
        first_w = row_taps(
            kernels,
            kernel_index,
            glob // 2,
            1 + parity,
            channel,
            jnp.ones((rows_here,), jnp.float32),
        )
        second_out = (glob + 1) // 2
        second_ok = ((parity == 1) & (second_out < total_out)).astype(jnp.float32)
        second_w = row_taps(
            kernels, kernel_index, second_out, jnp.zeros_like(glob), channel, second_ok
        )
        planes = jnp.stack([correlate(cycle, first_w), correlate(cycle, second_w)])
        back = lax.all_to_all(planes, "azimuth", split_axis=2, concat_axis=1, tiled=True)
        back = back.reshape(2, lat_half, 2, fields, lon_dev)
        near = back[0, :, 0] + back[0, :, 1]
        upper = back[1, :, 1]
        edge = shifted(upper[-1], "polar", 1)
        summed = near + jnp.concatenate([edge[None], upper[:-1]], axis=0)
        results.append(finish(summed, w_mix, w_in, b_in, w_out))
    return jnp.stack(results)


LANES = 128
SUB = 8
GROUP = 4
WIDE = 256
MESH = pl.DeviceIdType.MESH


def halves(x):
    top = x.astype(jnp.bfloat16).astype(jnp.float32)
    return top, x - top


def room_of(lon_dev):
    return -(-(lon_dev // 2 * GROUP) // 16) * 16


ERFC = (0.254829592, -0.284496736, 1.421413741, -1.453152027, 1.061405429)
ERFC_P = 0.3275911


def gelu(x):
    size = jnp.abs(x)
    base = size * (ERFC_P * 0.5**0.5) + 1.0
    guess = pl.reciprocal(base, approx=True)
    t = guess * (2.0 - base * guess)
    poly = ERFC[4] * 0.5
    for coefficient in ERFC[3::-1]:
        poly = poly * t + coefficient * 0.5
    upper = poly * t * jnp.exp2(x * x * (-0.5 / math.log(2.0)))
    return jnp.maximum(x, 0.0) - size * upper


def mlp_rows(fields, extra, left16, first, rest, second, held):
    chunks = first.shape[1] // WIDE
    at = 3 * fields + 3
    low_at = at + 2 * extra

    def act(weights):
        return gelu(jnp.dot(left16, weights, preferred_element_type=jnp.float32))

    total = None
    done = 0
    for c in range(chunks):
        hidden = act(first[:, c * WIDE : (c + 1) * WIDE])
        top = hidden.astype(jnp.bfloat16)
        low = (hidden - top.astype(jnp.float32)).astype(jnp.bfloat16)
        base = 3 * c * WIDE
        held[:, base : base + WIDE] = top
        held[:, base + WIDE : base + 2 * WIDE] = top
        held[:, base + 2 * WIDE : base + 3 * WIDE] = low
        if c == chunks - 1:
            top, low = halves(act(rest[...]))
            lane = lax.broadcasted_iota(jnp.int32, top.shape, 1)
            mixed = jnp.where(
                lane < at,
                left16.astype(jnp.float32),
                jnp.where(lane < low_at, top, jnp.where(lane < low_at + extra, low, 0.0)),
            )
            held[:, 3 * chunks * WIDE :] = mixed.astype(jnp.bfloat16)
        if c % 2 == 1 or c == chunks - 1:
            upto = base + 3 * WIDE if c < chunks - 1 else held.shape[1]
            term = jnp.dot(held[:, done:upto], second[done:upto, :], preferred_element_type=jnp.float32)
            total = term if total is None else total + term
            done = upto
    return total


def exchange(
    bands,
    columns,
    idx_ref,
    kern,
    w_mix,
    b_in,
    st_hbm,
    w_in_hbm,
    w_out_hbm,
    early_out,
    st,
    w_in,
    w_out,
    first,
    rest,
    second,
    left,
    rows_f32,
    held,
    result,
    peer,
    edge,
    blocks,
    taps,
    own,
    outgoing,
    incoming,
    load_sem,
    result_sem,
    peer_send,
    peer_recv,
    edge_send,
    edge_recv,
    relay_send,
    relay_recv,
    part_send,
    part_recv,
):
    members, lat_dev, fields, lon_dev = st.shape
    lat_half = lat_dev // 2
    tiles = fields // SUB
    embed, ffn = w_in.shape
    pieces = 2 * members
    az = lax.axis_index("azimuth")
    band = lax.axis_index("polar")
    core = lax.rem(az, 2)
    chip = az // 2
    chips = columns // 2
    mate = chip * 2 + 1 - core
    near = lax.rem(chip + chips - 1 + 2 * core, chips) * 2 + core
    far = lax.rem(chip + chips + 1 - 2 * core, chips) * 2 + core
    next_band = lax.rem(band + 1, bands)
    last_band = lax.rem(band + bands - 1, bands)

    loads = [pltpu.make_async_copy(st_hbm.at[m], st.at[m], load_sem.at[m]) for m in range(members)]
    load_in = pltpu.make_async_copy(w_in_hbm, w_in, load_sem.at[members])
    load_out = pltpu.make_async_copy(w_out_hbm, w_out, load_sem.at[members + 1])
    for copy in loads:
        copy.start()

    barrier = pltpu.get_barrier_semaphore()
    for who in ((band, mate), (band, near), (band, far), (last_band, az)):
        pl.semaphore_signal(barrier, inc=1, device_id=who, device_id_type=MESH)

    load_in.start()
    load_out.start()

    half = TAPS // 2
    pad = half - 1
    for o in range(lat_half):
        k = idx_ref[band * lat_half + o]
        for a in range(3):
            columns_of = kern[k, :, a, :].T
            if o == 0 and a == 0:
                columns_of = columns_of * jnp.where(band > 0, 1.0, 0.0)
            for t in range(TAPS):
                taps[o * 3 + a, t + pad] = jnp.broadcast_to(columns_of[:, t : t + 1], (fields, LANES))
            for t in range(pad):
                taps[o * 3 + a, t] = jnp.zeros((fields, LANES), jnp.float32)
                taps[o * 3 + a, t + pad + TAPS] = jnp.zeros((fields, LANES), jnp.float32)

    pl.semaphore_wait(barrier, 4)

    def remote(src, dst, send, recv, who):
        return pltpu.make_async_remote_copy(
            src_ref=src, dst_ref=dst, send_sem=send, recv_sem=recv, device_id=who, device_id_type=MESH
        )

    peers = []
    edges = []
    relays = []
    for m in range(members):
        peers.append(remote(st_hbm.at[m], peer.at[m], peer_send.at[m], peer_recv.at[m], (band, mate)))
        edges.append(
            remote(
                st_hbm.at[m, lat_dev - 1], edge.at[0, m], edge_send.at[m], edge_recv.at[m], (next_band, az)
            )
        )
        relays.append(
            remote(edge.at[0, m], edge.at[1, m], relay_send.at[m], relay_recv.at[m], (band, mate))
        )
    for m in range(members):
        edges[m].start()
        peers[m].start()

    spare = lon_dev - LANES

    def unpack(src, m, lat, to):
        x = src[:, :LANES]
        y = src[:, LANES:]
        y = jnp.concatenate([y, jnp.zeros((fields, LANES - spare), jnp.float32)], axis=1)
        lane = lax.broadcasted_iota(jnp.int32, x.shape, 1)
        blocks[m, lat, to] = x
        blocks[m, lat, to + 1] = pltpu.roll(jnp.where(lane < SPACING, y, x), LANES - SPACING, 1)

    turns = [q * SPACING % LANES for q in range(GROUP)]

    def pack(value, ref, at, rows):
        lane = lax.broadcasted_iota(jnp.int32, (SUB, LANES), 1)
        turned = [value[0]] + [pltpu.roll(value[q], turns[q], 1) for q in range(1, GROUP)]
        ref[at + (0, rows, slice(None))] = jnp.where(lane < turns[1], turned[0], turned[1])
        ref[at + (1, rows, slice(None))] = jnp.where(lane < turns[2], turned[1], turned[2])
        ref[at + (2, rows, slice(None))] = jnp.where(lane < turns[3], turned[2], turned[3])

    mine = 2 * core
    theirs = 2 - 2 * core
    plans = {
        "near": (2, mine, pad + 2 * half * (1 - core), lambda k: outgoing.at[0, k]),
        "far": (4, 0, pad + 2 * (half - 1) * core, lambda k: outgoing.at[1, k]),
        "own": (4, 0, pad + half - 2 * core, lambda k: own.at[k]),
    }

    def terms(x, tap, base, rows):
        w = {d: taps[tap, base + d, rows, :] for d in range(-1, len(x))}
        sums = []
        for j in range(2):
            term = w[-j] * x[0]
            for b in range(1, len(x)):
                term = term + w[b - j] * x[b]
            sums.append(term)
        return sums

    def correlate_part(m, plan, with_edge):
        width, start, base, ref_of = plans[plan]

        def body(r, carry):
            rows = pl.ds(pl.multiple_of(r * SUB, SUB), SUB)
            total = [[None] * lat_half for _ in range(2)]
            for o in range(lat_half):
                for a in range(1 if o == 0 and not with_edge else 0, 3):
                    x = [blocks[m, 2 * o + a, start + b, rows, :] for b in range(width)]
                    for j, term in enumerate(terms(x, o * 3 + a, base, rows)):
                        old = total[j][o]
                        total[j][o] = term if old is None else old + term
            for j in range(2):
                pack(total[j], ref_of(2 * m + j), (), rows)
            return carry

        lax.fori_loop(0, tiles, body, 0)

    def add_edge(m, plan):
        width, start, base, ref_of = plans[plan]

        def body(r, carry):
            rows = pl.ds(pl.multiple_of(r * SUB, SUB), SUB)
            lane = lax.broadcasted_iota(jnp.int32, (SUB, LANES), 1)
            x = [blocks[m, 0, start + b, rows, :] for b in range(width)]
            for j, term in enumerate(terms(x, 0, base, rows)):
                ref = ref_of(2 * m + j)
                ref[0, rows, :] = ref[0, rows, :] + jnp.where(lane < SPACING, term, 0.0)
            return carry

        lax.fori_loop(0, tiles, body, 0)

    def part(way, k):
        return remote(
            outgoing.at[way, k],
            incoming.at[way, k],
            part_send.at[way, k],
            part_recv.at[way, k],
            (band, (near, far)[way]),
        )

    for m in range(members):
        loads[m].wait()
        for lat in range(lat_dev):
            unpack(st.at[m, lat], m, lat + 1, mine)
        correlate_part(m, "near", False)
        edges[m].wait()
        relays[m].start()
        unpack(edge.at[0, m], m, 0, mine)
        add_edge(m, "near")
        if m == 0:
            for j in range(2):
                part(0, j).start()
        peers[m].wait()
        for lat in range(lat_dev):
            unpack(peer.at[m, lat], m, lat + 1, theirs)
        correlate_part(m, "far", False)
        relays[m].wait()
        unpack(edge.at[1, m], m, 0, theirs)
        add_edge(m, "far")
        if m == 0:
            for j in range(2):
                part(1, j).start()
    for m in range(members):
        correlate_part(m, "own", True)

    def follow(k):
        for way in range(2):
            part(way, k - 2).wait_send()
        for way in range(2):
            part(way, k).start()

    main = ffn // WIDE * WIDE
    extra = ffn - main
    at = 3 * fields + 3
    mix_top, mix_low = halves(w_mix[...])
    stacked = jnp.concatenate([mix_top, mix_low], axis=0).astype(jnp.bfloat16)
    load_in.wait()

    def product(cols):
        in_top, in_low = halves(w_in[:, cols])
        big = jnp.dot(stacked, in_top.astype(jnp.bfloat16), preferred_element_type=jnp.float32)
        small = jnp.dot(
            mix_top.astype(jnp.bfloat16), in_low.astype(jnp.bfloat16), preferred_element_type=jnp.float32
        )
        whole = big[:fields] + (big[fields:] + small)
        top, low = halves(whole)
        bias, leave = halves(b_in[cols][None, :])
        bias_low, leave = halves(leave)
        width = whole.shape[1]
        return jnp.concatenate(
            [top, low, top, bias, bias_low, leave, jnp.zeros((WIDE - at, width), jnp.float32)], axis=0
        )

    for c in range(main // WIDE):
        cols = slice(c * WIDE, (c + 1) * WIDE)
        first[:, cols] = product(cols).astype(jnp.bfloat16)
    tail = product(slice(main, ffn))
    rest[...] = jnp.concatenate(
        [jnp.zeros((WIDE, at), jnp.float32)]
        + [tail] * 3
        + [jnp.zeros((WIDE, WIDE - at - 3 * extra), jnp.float32)],
        axis=1,
    ).astype(jnp.bfloat16)
    follow(2)
    load_out.wait()
    for c in range(main // WIDE):
        top, low = halves(w_out[:, c * WIDE : (c + 1) * WIDE].T)
        base = 3 * c * WIDE
        second[base : base + WIDE, :] = top.astype(jnp.bfloat16)
        second[base + WIDE : base + 2 * WIDE, :] = low.astype(jnp.bfloat16)
        second[base + 2 * WIDE : base + 3 * WIDE, :] = top.astype(jnp.bfloat16)
    top, low = halves(w_out[:, main:].T)
    second[3 * main :, :] = jnp.concatenate(
        [mix_top, mix_low, mix_top, jnp.zeros((3, embed), jnp.float32), top, low, top]
        + [jnp.zeros((WIDE - at - 3 * extra, embed), jnp.float32)],
        axis=0,
    ).astype(jnp.bfloat16)

    for k in range(3, pieces):
        follow(k)
    count = lon_dev // 2
    room = rows_f32.shape[1]
    for side in range(WIDE // LANES):
        rows_f32[side, count * GROUP :, :] = jnp.zeros((room - count * GROUP, LANES), jnp.float32)

    def finish_part(k):
        for way in range(2):
            part(way, k).wait_recv()
        v = [own[k, i] + incoming[0, k, i] + incoming[1, k, i] for i in range(GROUP - 1)]
        lane = lax.broadcasted_iota(jnp.int32, v[0].shape, 1)
        fields_of = [v[0]]
        for q in range(1, GROUP):
            both = v[q - 1] if q == GROUP - 1 else jnp.where(lane >= turns[q], v[q - 1], v[q])
            fields_of.append(pltpu.roll(both, LANES - turns[q], 1))
        for q in range(GROUP):
            top, low = halves(fields_of[q])
            flat = jnp.concatenate(
                [top, top, low, jnp.ones((3, LANES), jnp.float32)]
                + [jnp.zeros((WIDE - at, LANES), jnp.float32)],
                axis=0,
            )
            turned = flat.T[:count]
            for side in range(WIDE // LANES):
                rows_f32[side, pl.ds(q, count, stride=GROUP), :] = turned[
                    :, side * LANES : (side + 1) * LANES
                ]
        return jnp.concatenate([rows_f32[side] for side in range(WIDE // LANES)], axis=1).astype(
            jnp.bfloat16
        )

    def store_of(k):
        return pltpu.make_async_copy(result, early_out.at[k], result_sem)

    def piece(k, carry):
        left[...] = finish_part(k)
        total = mlp_rows(fields, extra, left[...], first, rest, second, held)

        @pl.when(k > 0)
        def _():
            store_of(k - 1).wait()

        result[...] = total[: count * GROUP].reshape(count, GROUP, embed)
        store_of(k).start()
        return carry

    lax.fori_loop(0, pieces, piece, 0)
    for k in range(pieces - 2, pieces):
        for way in range(2):
            part(way, k).wait_send()
    store_of(pieces - 1).wait()


def deliver(cuts, made, out, passing, in_sem, out_sem):
    pieces, count = made.shape[:2]
    step = count // cuts
    inward = []
    outward = []
    for k in range(pieces):
        for c in range(cuts):
            rows = pl.ds(c * step, step)
            i = k * cuts + c
            inward.append(pltpu.make_async_copy(made.at[k, rows], passing.at[k, rows], in_sem.at[i]))
            outward.append(
                pltpu.make_async_copy(
                    passing.at[k, rows],
                    out.at[k // 2, pl.ds(k % 2 * count + c * step, step)],
                    out_sem.at[i],
                )
            )
    for copy in inward:
        copy.start()
    for come, go in zip(inward, outward):
        come.wait()
        go.start()
    for copy in outward:
        copy.wait()


def per_device_fast(bands, columns, state, kernels, kernel_index, w_mix, w_in, b_in, w_out):
    members, lat_dev, fields, lon_dev = state.shape
    lat_half = lat_dev // 2
    pieces = 2 * members
    count = lon_dev // 2
    embed, ffn = w_in.shape
    main = ffn // WIDE * WIDE
    depth = 3 * main + WIDE
    room = room_of(lon_dev)
    vmem = pl.BlockSpec(memory_space=pltpu.VMEM)
    hbm = pl.BlockSpec(memory_space=pl.ANY)
    f32 = jnp.float32
    half = jnp.bfloat16
    dma = pltpu.SemaphoreType.DMA
    packed = (pieces, GROUP - 1, fields, LANES)
    made = pl.pallas_call(
        functools.partial(exchange, bands, columns),
        out_shape=jax.ShapeDtypeStruct((pieces, count, GROUP, embed), f32),
        in_specs=[pl.BlockSpec(memory_space=pltpu.SMEM)] + [vmem] * 3 + [hbm] * 3,
        out_specs=hbm,
        scratch_shapes=[
            pltpu.VMEM(state.shape, f32),
            pltpu.VMEM(w_in.shape, f32),
            pltpu.VMEM(w_out.shape[::-1], f32),
            pltpu.VMEM((WIDE, main), half),
            pltpu.VMEM((WIDE, WIDE), half),
            pltpu.VMEM((depth, embed), half),
            pltpu.VMEM((room, WIDE), half),
            pltpu.VMEM((WIDE // LANES, room, LANES), f32),
            pltpu.VMEM((room, depth), half),
            pltpu.VMEM((count, GROUP, embed), f32),
            pltpu.VMEM(state.shape, f32),
            pltpu.VMEM((2, members, fields, lon_dev), f32),
            pltpu.VMEM((members, lat_dev + 1, 4, fields, LANES), f32),
            pltpu.VMEM((lat_half * 3, 2 * TAPS - 3, fields, LANES), f32),
            pltpu.VMEM(packed, f32),
            pltpu.VMEM((2,) + packed, f32),
            pltpu.VMEM((2,) + packed, f32),
            dma((members + 2,)),
            dma(()),
            dma((members,)),
            dma((members,)),
            dma((members,)),
            dma((members,)),
            dma((members,)),
            dma((members,)),
            dma((2, pieces)),
            dma((2, pieces)),
        ],
        compiler_params=pltpu.CompilerParams(
            collective_id=0, has_side_effects=True, vmem_limit_bytes=60 * 2**20
        ),
        name="exchange",
    )(
        kernel_index,
        jnp.transpose(kernels, (0, 2, 1, 3)),
        w_mix,
        b_in,
        state,
        w_in,
        w_out.T,
    )
    cuts = 1
    out = pl.pallas_call(
        functools.partial(deliver, cuts),
        out_shape=jax.ShapeDtypeStruct((members, lon_dev, lat_half, embed), f32),
        in_specs=[hbm],
        out_specs=hbm,
        scratch_shapes=[
            pltpu.VMEM((pieces, count, GROUP, embed), f32),
            dma((pieces * cuts,)),
            dma((pieces * cuts,)),
        ],
        compiler_params=pltpu.CompilerParams(vmem_limit_bytes=60 * 2**20),
        name="deliver",
    )(made)
    return jnp.transpose(out, (0, 2, 1, 3))


def fits(mesh, state, w_in):
    bands, columns = mesh.shape["polar"], mesh.shape["azimuth"]
    members, lat, fields, lon = state.shape
    main = w_in.shape[1] // WIDE * WIDE
    return (
        bands >= 2
        and columns % 2 == 0
        and columns >= 6
        and lon == 2 * SPACING * columns
        and lat == 2 * GROUP * bands
        and fields % SUB == 0
        and main > 0
        and 3 * fields + 3 + 3 * (w_in.shape[1] - main) <= WIDE
    )


def solution(mesh):
    placed = (P(None, "polar", None, "azimuth"), P(), P(), P(), P(), P(), P())

    def run(state, kernels, kernel_index, w_mix, w_in, b_in, w_out):
        body = per_device
        if fits(mesh, state, w_in):
            body = functools.partial(per_device_fast, mesh.shape["polar"], mesh.shape["azimuth"])
        return jax.shard_map(
            body,
            mesh=mesh,
            in_specs=placed,
            out_specs=P(None, "polar", "azimuth", None),
            check_vma=False,
        )(state, kernels, kernel_index, w_mix, w_in, b_in, w_out)

    return run
```
